32 devices in a mesh: case: 2 (over y), wall: 4 (over z), azim: 4 (over x, core).
Axes of the slice: x: 2, y: 2, z: 4, core: 2. Of those that a mesh axis runs over, the one named last changes fastest.
Arguments:
- state: float32 [12, 2, 32, 512], P(None, 'case', 'wall', 'azim'), parts along dimension 1, may hold values from 0.5 to 1.5
- courant: float32 [2, 32, 512], P('case', 'wall', 'azim'), parts along dimension 0, may hold values from -0.6 to 0.6
- cross_sections: float32 [64], replicated, may hold values from 0.02 to 0.6
- band_fractions: float32 [64], replicated, may hold values from 0.02 to 0.2
- absorb_index: int32 [11, 16], replicated, may hold values from 0 to 63
- band_index: int32 [16], replicated, may hold values from 0 to 63
Outputs:
- new_state: float32 [12, 2, 32, 512], P(None, 'case', 'wall', 'azim'), parts along dimension 1
- wall_flux: float32 [2, 512], P('case', 'azim'), parts along dimension 0
The draws below stay inside these ranges and needn't reach their ends.
There are 2 independent parts, one for each index of `case`. The reference program is written for one: setup_inputs(seed, part) draws one part's arguments, and reference() takes and returns one part's arrays. A program takes and returns all parts, laid end to end along the dimension named above; an argument that names none is the same for every part. Nothing has to cross between parts.
All inputs are finite; a program needn't handle non-finite values.
Results may differ from the reference program's by a relative error of at most 0.0003.
Values sent between devices are 32-bit elements; how exact they have to be, the bound alone decides.
A program may use at most 64 MiB of HBM per device.

```python
import math
import jax
import jax.numpy as jnp
from jax import lax

STATIONS = 1
BANDS = 16
SPECIES = 11
NTAB = 64
COMPS = 12
NR = 32
NA = 512


def touch_ends(drawn, stream_key, low, largest):
    index_at = [jax.random.randint(jax.random.fold_in(stream_key, axis), (), 0, length) for axis, length in enumerate(drawn.shape)]
    main_axis = drawn.shape.index(max(drawn.shape))
    next_to = index_at[:main_axis] + [(index_at[main_axis] + 1) % drawn.shape[main_axis]] + index_at[main_axis + 1:]
    return drawn.at[tuple(index_at)].set(low).at[tuple(next_to)].set(largest)


def steps_of(stream_key, extent, pieces, least, high):
    factor_of, own = 1.0, jax.random.fold_in(stream_key, 6)
    for position, blocks in pieces:
        draws = jnp.exp(jax.random.uniform(jax.random.fold_in(own, position), (blocks,), jnp.float32, least / len(pieces), high / len(pieces)))
        factor_of = factor_of * jnp.repeat(draws, extent[position] // blocks).reshape([-1 if axis == position else 1 for axis in range(len(extent))])
    return factor_of


def setup_inputs(seed: int = 0, part: int = 0) -> dict:
    arg_keys = jax.random.split(jax.random.key(seed), 7)
    own_keys = jax.random.split(jax.random.fold_in(arg_keys[6], part), 7)
    return {
        "state": jnp.clip(0.5 + 1.0 * jax.random.uniform(own_keys[0], (COMPS, STATIONS, NR, NA), jnp.float32) ** steps_of(own_keys[0], (COMPS, STATIONS, NR, NA), ((2, 4), (3, 4)), -0.2, 0.2), 0.5, 1.5),
        "courant": jnp.clip(jax.random.uniform(own_keys[1], (STATIONS, NR, NA), jnp.float32, -0.6, 0.6) * steps_of(own_keys[1], (STATIONS, NR, NA), ((1, 4), (2, 4)), -0.4, 0.0), -0.6, 0.6),
        "cross_sections": jnp.clip(jnp.exp(jax.random.uniform(arg_keys[2], (NTAB,), jnp.float32, math.log(0.02), math.log(0.6))), 0.02, 0.6),
        "band_fractions": jnp.clip(jnp.exp(jax.random.uniform(arg_keys[3], (NTAB,), jnp.float32, math.log(0.02), math.log(0.2))), 0.02, 0.2),
        "absorb_index": touch_ends(jax.random.randint(arg_keys[4], (SPECIES, BANDS), 0, NTAB), jax.random.fold_in(arg_keys[4], 1), 0, NTAB - 1).astype(jnp.int32),
        "band_index": touch_ends(jax.random.randint(arg_keys[5], (BANDS,), 0, NTAB), jax.random.fold_in(arg_keys[5], 1), 0, NTAB - 1).astype(jnp.int32),
    }


KERNEL_WEIGHTS = (0.55, 0.45)
KERNEL_RATES = (1.15, 3.4)
FILTER_STRENGTH = 0.02
COUPLING = 0.1


def band_tables(absorb_index, band_index, cross_sections, band_fractions):
    entries = cross_sections.shape[0]
    table_slots = lax.broadcasted_iota(jnp.int32, (1, 1, entries), 2)
    spectral_absorber_area = jnp.sum(jnp.where(absorb_index[:, :, None] == table_slots, cross_sections[None, None, :], 0.0), axis=2)
    chosen_values = jnp.where(band_index[:, None] == table_slots[0], band_fractions[None, :], 0.0)
    return spectral_absorber_area, jnp.sum(chosen_values, axis=1)


def viewing_line_irradiance(kinetic_heat_level, species_concentrations, spectral_absorber_area, spectral_fraction_weight, mesh_cell_width, viewing_line_dimension):
    absorption = jnp.einsum("kb,kij->bij", spectral_absorber_area, species_concentrations, precision=lax.Precision.HIGHEST)
    optical_thickness_step = absorption * mesh_cell_width
    optical_depth = lax.cumsum(optical_thickness_step, viewing_line_dimension) - 0.5 * optical_thickness_step
    radiated_energy_rate = spectral_fraction_weight[:, None, None] * kinetic_heat_level[None] ** 4 * optical_thickness_step
    net_flux = 0.0
    wall_flux = 0.0
    for weight, decay_rate in zip(KERNEL_WEIGHTS, KERNEL_RATES):
        growth = jnp.exp(decay_rate * optical_depth)
        falloff = jnp.exp(-decay_rate * optical_depth)
        upward = falloff * lax.cumsum(radiated_energy_rate * growth, viewing_line_dimension)
        tail_sum = lax.cumsum(radiated_energy_rate * falloff, viewing_line_dimension, reverse=True)
        net_flux = net_flux + weight * jnp.sum(upward - growth * tail_sum, axis=0)
        wall_flux = wall_flux + weight * jnp.sum(lax.index_in_dim(tail_sum, 0, viewing_line_dimension, keepdims=False), axis=0)
    return net_flux, wall_flux


def edge_pad(net_flux, viewing_line_dimension):
    count = net_flux.shape[viewing_line_dimension]
    first_row = lax.slice_in_dim(net_flux, 0, 1, axis=viewing_line_dimension)
    last_row = lax.slice_in_dim(net_flux, count - 1, count, axis=viewing_line_dimension)
    return jnp.concatenate([first_row, net_flux, last_row], viewing_line_dimension)


def divergence(padded, viewing_line_dimension, mesh_cell_width):
    count = padded.shape[viewing_line_dimension] - 2
    before = lax.slice_in_dim(padded, 0, count, axis=viewing_line_dimension)
    after = lax.slice_in_dim(padded, 2, count + 2, axis=viewing_line_dimension)
    return (before - after) / (2.0 * mesh_cell_width)


def tendency(shifted, courant, heating):
    gradient = (45.0 * (shifted(1) - shifted(-1)) - 9.0 * (shifted(2) - shifted(-2)) + (shifted(3) - shifted(-3))) / 60.0
    smoothing = shifted(-3) + shifted(3) - 6.0 * (shifted(-2) + shifted(2)) + 15.0 * (shifted(-1) + shifted(1)) - 20.0 * shifted(0)
    change_sum = FILTER_STRENGTH * smoothing - courant[None] * gradient
    return change_sum.at[0].add(COUPLING * heating)


def reference(state, courant, cross_sections, band_fractions, absorb_index, band_index):
    spectral_absorber_area, spectral_fraction_weight = band_tables(absorb_index, band_index, cross_sections, band_fractions)
    mesh_cell_width = 1.0 / NR

    def segment_change(current):
        components = current.shape[0]
        line_data = jnp.transpose(current, (0, 2, 1, 3)).reshape(components, NR, STATIONS * NA)
        net_flux, wall_flux = viewing_line_irradiance(line_data[0], line_data[1:], spectral_absorber_area, spectral_fraction_weight, mesh_cell_width, 1)
        heating = divergence(edge_pad(net_flux, 0), 0, mesh_cell_width)
        heating = jnp.transpose(heating.reshape(NR, STATIONS, NA), (1, 0, 2))

        def shifted(offset):
            return jnp.roll(current, -offset, axis=3)

        return tendency(shifted, courant, heating), wall_flux.reshape(STATIONS, NA)

    first_change, first_flux = segment_change(state)
    middle = state + first_change
    second_change, second_flux = segment_change(middle)
    new_state = 0.5 * (state + middle + second_change)
    return new_state, 0.5 * (first_flux + second_flux)
```

```python
import functools

import jax
import jax.numpy as jnp
from jax import lax
from jax.experimental import pallas as pl
from jax.experimental.pallas import tpu as pltpu
from jax.sharding import PartitionSpec as P

WEIGHTS = (0.55, 0.45)
RATES = (1.15, 3.4)
FILTER = 0.02
COUPLING = 0.1
REACH = 6
MESH = pl.DeviceIdType.MESH
EXACT = lax.Precision.HIGHEST


def loop(count, body, init):
    if count <= 4:
        for i in range(count):
            init = body(i, init)
        return init
    return lax.fori_loop(0, count, body, init)


def kernel(
    walls, azims, state, courant, sections, fractions, absorb, band,
    new_state, wall_out,
    gs, gc, gl, gr, ms, mh, edge_l, edge_r,
    em, t1, t2, em_h, t1_h, t2_h, em_m, t1_m, t2_m, net, net_h,
    table, idx, cs, bf, bi,
    local_sem, s_state, r_state, s_cour, r_cour, s_edge, r_edge, ready,
):
    comps, rows, lanes = state.shape
    species, bands = absorb.shape
    entries = sections.shape[0]
    total = rows * walls
    f32, bf16 = jnp.float32, jnp.bfloat16
    me = lax.axis_index("wall")
    az = lax.axis_index("azim")
    right, left = lax.rem(az + 1, azims), lax.rem(az + azims - 1, azims)
    sides = (right, left)
    first = ((az == azims - 1) | (az % 2 == 0), (left % 2 == 1) & (left != azims - 1))

    def peer(d):
        return lax.rem(me + d, walls)

    barrier = pltpu.get_barrier_semaphore()

    def greet(i, _):
        z = peer(i + 1)

        @pl.when(z > me)
        def _later():
            pl.semaphore_signal(barrier, inc=1, device_id={"wall": z}, device_id_type=MESH)
            for side in sides:
                pl.semaphore_signal(barrier, inc=1, device_id={"wall": z, "azim": side}, device_id_type=MESH)

        return 0

    loop(walls - 1, greet, 0)
    for i in range(2):

        @pl.when(jnp.logical_not(first[i]))
        def _later():
            pl.semaphore_signal(barrier, inc=1, device_id={"azim": sides[i]}, device_id_type=MESH)

    loads = [
        pltpu.make_async_copy(src, dst, local_sem.at[i])
        for i, (src, dst) in enumerate(
            [(state, gs.at[me]), (courant, gc.at[me]), (sections, cs), (fractions, bf), (absorb, idx), (band, bi)]
        )
    ]
    for c in loads:
        c.start()

    greeters = 3 * me + first[0].astype(jnp.int32) + first[1].astype(jnp.int32)

    @pl.when(greeters > 0)
    def _greeted():
        pl.semaphore_wait(barrier, greeters)


    def state_copy(d, slot):
        return pltpu.make_async_remote_copy(
            src_ref=state, dst_ref=gs.at[slot], send_sem=s_state.at[d], recv_sem=r_state.at[d],
            device_id={"wall": peer(d)}, device_id_type=MESH)

    def line_copy(d, slot):
        return pltpu.make_async_remote_copy(
            src_ref=courant, dst_ref=gc.at[slot], send_sem=s_cour.at[d], recv_sem=r_cour.at[d],
            device_id={"wall": peer(d)}, device_id_type=MESH)

    def edge_copy(i, d, slot):
        src, dst = ((edge_r, gl), (edge_l, gr))[i]
        return pltpu.make_async_remote_copy(
            src_ref=src, dst_ref=dst.at[slot], send_sem=s_edge.at[i, d], recv_sem=r_edge.at[i, d],
            device_id={"wall": peer(d), "azim": sides[i]}, device_id_type=MESH)

    def edge_copies(d, slot):
        return [edge_copy(i, d, slot) for i in range(2)]

    def state_first(i, _):
        z = peer(i + 1)

        @pl.when((z < me) & (z == 0))
        def _earliest():
            state_copy(i + 1, me).start()
            line_copy(i + 1, me).start()

        return 0

    def say_ready(i, _):
        z = peer(i + 1)

        @pl.when(z < me)
        def _earlier():
            pl.semaphore_signal(ready.at[0, me], inc=1, device_id={"wall": z}, device_id_type=MESH)
            for k, side in enumerate(sides):
                pl.semaphore_signal(ready.at[2 - k, me], inc=1, device_id={"wall": z, "azim": side}, device_id_type=MESH)

        return 0

    def rest_back(i, _):
        z = peer(i + 1)

        @pl.when((z < me) & (z > 0))
        def _earlier():
            state_copy(i, me).wait_send()
            state_copy(i + 1, me).start()
            line_copy(i + 1, me).start()

        @pl.when(z < me)
        def _edges():
            for c in edge_copies(i + 1, me):
                c.start()

        return 0

    def send_on(i, _):
        z = peer(i + 1)

        @pl.when(z > me)
        def _later():
            pl.semaphore_wait(ready.at[0, z], 1)
            state_copy(i + 1, me).start()
            line_copy(i + 1, me).start()
            for k in range(2):
                pl.semaphore_wait(ready.at[1 + k, z], 1)
                edge_copy(k, i + 1, me).start()

        return 0

    loop(walls - 1, state_first, 0)
    loop(walls - 1, say_ready, 0)
    for i in range(2):

        @pl.when(first[i])
        def _earlier():
            pl.semaphore_signal(ready.at[2 - i, me], inc=1, device_id={"azim": sides[i]}, device_id_type=MESH)

    for c in loads[:2]:
        c.wait()
    lane = lax.broadcasted_iota(jnp.int32, (rows, lanes), 1)
    el = jnp.zeros((rows, lanes), f32)
    er = jnp.zeros((rows, lanes), f32)
    for c in range(comps + 1):
        x = gs[me, c] if c < comps else gc[me]
        here = (lane >= REACH * c) & (lane < REACH * (c + 1))
        el = jnp.where(here, pltpu.roll(x, REACH * c, 1) if c else x, el)
        er = jnp.where(here, pltpu.roll(x, (REACH * (c + 1)) % lanes, 1), er)
    edge_l[...] = el
    edge_r[...] = er
    loop(walls - 1, rest_back, 0)
    for i in range(2):

        @pl.when(first[i])
        def _earlier():
            edge_copy(i, 0, me).start()


    for c in loads[2:]:
        c.wait()
    index = idx[...]
    picked = lax.fori_loop(
        0, entries, lambda t, acc: jnp.where(index == t, cs[t], acc), jnp.zeros((species, bands), f32), unroll=8)
    table[...] = jnp.zeros_like(table)
    table[0:species, 0:bands] = picked
    kpad = table.shape[0]
    rb = rows * bands
    cr = comps * rows
    spread = jnp.where(
        lax.broadcasted_iota(jnp.int32, (rb, lanes), 0) & (bands - 1) == lax.broadcasted_iota(jnp.int32, (rb, lanes), 1), 1.0, 0.0)
    by_row = lax.dot_general(spread, table[...], (((1,), (1,)), ((), ())), precision=EXACT, preferred_element_type=f32)
    columns = jnp.where(
        lax.broadcasted_iota(jnp.int32, (kpad, cr), 1) // rows == lax.broadcasted_iota(jnp.int32, (kpad, cr), 0) + 1, 1.0, 0.0)
    full = jnp.dot(by_row, columns, precision=EXACT, preferred_element_type=f32)
    same_row = lax.broadcasted_iota(jnp.int32, (rb, cr), 0) // bands == lax.broadcasted_iota(jnp.int32, (rb, cr), 1) % rows
    mat = jnp.where(same_row, full, 0.0) * (1.0 / total)
    mat_hi = mat.astype(bf16)
    mat_lo = (mat - mat_hi.astype(f32)).astype(bf16)
    mats = jnp.concatenate(
        [jnp.concatenate([mat_hi, mat_hi], axis=1), jnp.concatenate([mat_lo, mat_lo], axis=1)], axis=0)
    band_row = lax.broadcasted_iota(jnp.int32, (bands, lanes), 0)
    share = jnp.zeros((bands, lanes), f32)
    for b in range(bands):
        share = jnp.where(band_row == b, bf[bi[b]], share)
    share = share * WEIGHTS[0]
    heat_scale = COUPLING * total / 2.0

    def steps(values):
        u = values.reshape(cr, lanes)
        hi = u.astype(bf16)
        lo = (u - hi.astype(f32)).astype(bf16)
        both = jnp.dot(mats, jnp.concatenate([hi, lo], axis=0), preferred_element_type=f32)
        return both[:rb] + both[rb:]

    def fill(z, values, to_em, to_1, to_2, hot):
        step = steps(values)
        to_1[z] = jnp.exp(step * (-0.5 * RATES[0]))
        to_2[z] = jnp.exp(step * (-0.5 * RATES[1]))
        if hot:
            t = fourth(values[0])
        for r in range(rows):
            part = slice(r * bands, (r + 1) * bands)
            to_em[z, part] = step[part] * (share * t[r : r + 1] if hot else share)

    def fourth(t):
        t = t * t
        return t * t

    def fold(a):
        s = a[0:8]
        for k in range(8, bands, 8):
            s = s + a[k : k + 8]
        return s

    def scan(sets):
        zero = jnp.zeros((bands, lanes), f32)
        ratio = WEIGHTS[1] / WEIGHTS[0]
        n = len(sets)

        def up(z, carry):
            carry = list(carry)
            for r in range(rows):
                part = slice(r * bands, (r + 1) * bands)
                for i, (src, a, b, out) in enumerate(sets):
                    u1, u2, a1, a2 = carry[i]
                    e, b1, b2 = src[z, part], a[z, part], b[z, part]
                    u1 = e + (a1 * b1) * u1
                    u2 = ratio * e + (a2 * b2) * u2
                    out[1 + z * rows + r] = fold(u1 + u2)
                    carry[i] = (u1, u2, b1, b2)
            return tuple(carry)

        def down(k, carry):
            carry = list(carry)
            z = walls - 1 - k
            for r in reversed(range(rows)):
                part = slice(r * bands, (r + 1) * bands)
                for i, (src, a, b, out) in enumerate(sets):
                    d1, d2, a1, a2 = carry[i]
                    e, b1, b2 = src[z, part], a[z, part], b[z, part]
                    d1 = e + (a1 * b1) * d1
                    d2 = ratio * e + (a2 * b2) * d2
                    at = 1 + z * rows + r
                    out[at] = out[at] - fold(d1 + d2)
                    carry[i] = (d1, d2, b1, b2)
            return tuple(carry)

        start = ((zero,) * 4,) * n
        loop(walls, up, start)
        ends = loop(walls, down, start)
        for _s, _a, _b, out in sets:
            out[0] = out[1]
            out[total + 1] = out[total]
        d1, d2, a1, a2 = ends[0]
        return jnp.sum(fold(a1 * d1 + a2 * d2), axis=0, keepdims=True)

    sub = lax.broadcasted_iota(jnp.int32, (rows, lanes), 0)

    def heat(ref, z):
        at = z * rows
        a = [ref[at + i] - ref[at + i + 2] for i in range(rows)]
        order = [4 * ((s >> 2) & 1) + 2 * (1 - ((s >> 1) & 1)) + (1 - (s & 1)) for s in range(8)]
        a = [a[order.index(i)] for i in range(8)]
        low = sub < 4
        b = [jnp.where(low, a[i], a[i + 4]) + pltpu.roll(jnp.where(low, a[i + 4], a[i]), 4, 0) for i in range(4)]
        low = (sub & 3) < 2
        c = [
            jnp.where(low, b[i + 2] + pltpu.roll(b[i + 2], rows - 2, 0), b[i] + pltpu.roll(b[i], 2, 0))
            for i in range(2)
        ]
        low = (sub & 1) < 1
        d = jnp.where(low, c[1] + pltpu.roll(c[1], rows - 1, 0), c[0] + pltpu.roll(c[0], 1, 0))
        return heat_scale * d

    def around(x, h):
        s = {0: x}
        for o in (1, 2, 3):
            s[o] = pltpu.roll(jnp.where(lane >= o, x, h), lanes - o, 1)
            s[-o] = pltpu.roll(jnp.where(lane < lanes - o, x, h), o, 1)
        return s

    def tendency(s, cour):
        gradient = (45.0 / 60.0) * (s[1] - s[-1]) - (9.0 / 60.0) * (s[2] - s[-2]) + (1.0 / 60.0) * (s[3] - s[-3])
        smooth = (s[-3] + s[3]) - 6.0 * (s[-2] + s[2]) + 15.0 * (s[-1] + s[1]) - 20.0 * s[0]
        return FILTER * smooth - cour * gradient

    left_half = lane < lanes // 2

    def halo_of(pr, pk, c):
        a = pltpu.roll(pr, lanes - REACH * c, 1) if c else pr
        return jnp.where(left_half, a, pltpu.roll(pk, lanes - REACH * (c + 1), 1))

    def block(z):
        x = gs[z]
        fill(z, x, em, t1, t2, True)
        pr, pk = gr[z], gl[z]
        h = [halo_of(pr, pk, c) for c in range(comps)]
        fill(z, jnp.stack(h), em_h, t1_h, t2_h, True)
        cour = gc[z]
        m = [x[c] + tendency(around(x[c], h[c]), cour) for c in range(comps)]
        m = jnp.stack(m)
        ms[z] = m
        fill(z, m, em_m, t1_m, t2_m, False)

    for i in range(2):

        @pl.when(jnp.logical_not(first[i]))
        def _later():
            pl.semaphore_wait(ready.at[1 + i, me], 1)
            edge_copy(i, 0, me).start()

    loop(walls - 1, send_on, 0)
    for c in edge_copies(0, me):
        c.wait_recv()
    block(me)
    pr, pk = gr[me], gl[me]
    hc = halo_of(pr, pk, comps)
    cour = gc[me]
    for c in range(comps):
        h = halo_of(pr, pk, c)
        x = gs[me, c]
        mh[c] = h + tendency(around(h, x), hc)
        if c:
            m = ms[me, c]
            new_state[c] = 0.5 * (x + m + tendency(around(m, mh[c]), cour))

    def arrive(i, _):
        z = peer(i + 1)
        d = walls - 1 - i
        state_copy(d, z).wait_recv()
        line_copy(d, z).wait_recv()
        for c in edge_copies(d, z):
            c.wait_recv()
        block(z)
        return 0

    lax.fori_loop(0, walls - 1, arrive, 0)
    flux = scan([(em, t1, t2, net), (em_h, t1_h, t2_h, net_h)])

    def middle(z, _):
        m = ms[z, 0] + heat(net, z)
        ms[z, 0] = m
        t = fourth(m)
        for r in range(rows):
            part = slice(r * bands, (r + 1) * bands)
            em_m[z, part] = em_m[z, part] * t[r : r + 1]
        return 0

    loop(walls, middle, 0)
    flux = flux + scan([(em_m, t1_m, t2_m, net)])
    wall_out[...] = 0.5 * flux
    m = ms[me, 0]
    h = mh[0] + heat(net_h, me)
    new_state[0] = 0.5 * (gs[me, 0] + m + tendency(around(m, h), cour) + heat(net, me))

    def finish(i, _):
        nxt = peer(i + 2)

        @pl.when(jnp.logical_not((nxt < me) & (nxt > 0)))
        def _last():
            state_copy(i + 1, me).wait_send()

        line_copy(i + 1, me).wait_send()
        for c in edge_copies(i + 1, me):
            c.wait_send()
        return 0

    loop(walls - 1, finish, 0)
    for c in edge_copies(0, me):
        c.wait_send()


def hand_over(a, b, a_out, b_out, sems):
    copies = [pltpu.make_async_copy(a, a_out, sems.at[0]), pltpu.make_async_copy(b, b_out, sems.at[1])]
    for c in copies:
        c.start()
    for c in copies:
        c.wait()


def local(walls, azims, state, courant, cross_sections, band_fractions, absorb_index, band_index):
    comps, stations, rows, lanes = state.shape
    bands = absorb_index.shape[1]
    species = absorb_index.shape[0]
    entries = cross_sections.shape[0]
    total = rows * walls
    f32 = jnp.float32
    vmem = pltpu.VMEM
    dma = pltpu.SemaphoreType.DMA
    hbm_spec = pl.BlockSpec(memory_space=pltpu.HBM)
    vmem_spec = pl.BlockSpec(memory_space=pltpu.VMEM)
    new_state, wall = pl.pallas_call(
        functools.partial(kernel, walls, azims),
        out_shape=(
            pltpu.VMEM((comps, rows, lanes), f32),
            pltpu.VMEM((1, lanes), f32),
        ),
        in_specs=[hbm_spec] * 6,
        out_specs=(vmem_spec, vmem_spec),
        scratch_shapes=[
            vmem((walls, comps, rows, lanes), f32),
            vmem((walls, rows, lanes), f32),
            vmem((walls, rows, lanes), f32),
            vmem((walls, rows, lanes), f32),
            vmem((walls, comps, rows, lanes), f32),
            vmem((comps, rows, lanes), f32),
            vmem((rows, lanes), f32),
            vmem((rows, lanes), f32),
        ] + [vmem((walls, rows * bands, lanes), f32)] * 9 + [
            vmem((total + 2, 8, lanes), f32),
            vmem((total + 2, 8, lanes), f32),
            vmem((16, lanes), f32),
            vmem((species, bands), jnp.int32),
            pltpu.SMEM((entries,), f32),
            pltpu.SMEM((entries,), f32),
            pltpu.SMEM((bands,), jnp.int32),
            dma((6,)),
        ] + [dma((walls,))] * 4 + [dma((2, walls))] * 2 + [pltpu.SemaphoreType.REGULAR((3, walls))],
        compiler_params=pltpu.CompilerParams(
            collective_id=0, has_side_effects=True, vmem_limit_bytes=58 * 1024 * 1024),
    )(state.reshape(comps, rows, lanes), courant.reshape(rows, lanes), cross_sections, band_fractions, absorb_index, band_index)
    hbm = pl.BlockSpec(memory_space=pltpu.HBM)
    new_state, wall = pl.pallas_call(
        hand_over,
        out_shape=(
            jax.ShapeDtypeStruct((comps, rows, lanes), f32),
            jax.ShapeDtypeStruct((1, lanes), f32),
        ),
        in_specs=[pl.BlockSpec(memory_space=pl.ANY)] * 2,
        out_specs=(hbm, hbm),
        scratch_shapes=[dma((2,))],
    )(pltpu.with_memory_space_constraint(new_state, pltpu.VMEM), pltpu.with_memory_space_constraint(wall, pltpu.VMEM))
    return new_state.reshape(state.shape), wall


def solution(mesh):
    return jax.shard_map(
        functools.partial(local, mesh.shape["wall"], mesh.shape["azim"]),
        mesh=mesh,
        in_specs=(P(None, "case", "wall", "azim"), P("case", "wall", "azim"), P(), P(), P(), P()),
        out_specs=(P(None, "case", "wall", "azim"), P("case", "azim")),
        check_vma=False,
    )
```

```python
import functools

import jax
import jax.numpy as jnp
from jax import lax
from jax.experimental import pallas as pl
from jax.experimental.pallas import tpu as pltpu
from jax.sharding import PartitionSpec as P

WEIGHTS = (0.55, 0.45)
RATES = (1.15, 3.4)
FILTER = 0.02
COUPLING = 0.1
REACH = 6
MESH = pl.DeviceIdType.MESH
EXACT = lax.Precision.HIGHEST


def loop(count, body, init):
    if count <= 4:
        for i in range(count):
            init = body(i, init)
        return init
    return lax.fori_loop(0, count, body, init)


def kernel(
    walls, azims, state, courant, sections, fractions, absorb, band,
    new_state, wall_out,
    gs, gc, gl, gr, ms, mh, edge_l, edge_r,
    em, t1, t2, em_h, t1_h, t2_h, em_m, t1_m, t2_m, net, net_h,
    table, col, idx, cs, bf, bi,
    local_sem, s_state, r_state, s_cour, r_cour, s_edge, r_edge, ready,
):
    comps, rows, lanes = state.shape
    species, bands = absorb.shape
    entries = sections.shape[0]
    total = rows * walls
    f32 = jnp.float32
    me = lax.axis_index("wall")
    az = lax.axis_index("azim")
    right, left = lax.rem(az + 1, azims), lax.rem(az + azims - 1, azims)
    sides = (right, left)
    first = ((az == azims - 1) | (az % 2 == 0), (left % 2 == 1) & (left != azims - 1))

    def peer(d):
        return lax.rem(me + d, walls)

    barrier = pltpu.get_barrier_semaphore()

    def greet(i, _):
        z = peer(i + 1)

        @pl.when(z > me)
        def _later():
            pl.semaphore_signal(barrier, inc=1, device_id={"wall": z}, device_id_type=MESH)
            for side in sides:
                pl.semaphore_signal(barrier, inc=1, device_id={"wall": z, "azim": side}, device_id_type=MESH)

        return 0

    loop(walls - 1, greet, 0)
    for i in range(2):

        @pl.when(jnp.logical_not(first[i]))
        def _later():
            pl.semaphore_signal(barrier, inc=1, device_id={"azim": sides[i]}, device_id_type=MESH)

    loads = [
        pltpu.make_async_copy(src, dst, local_sem.at[i])
        for i, (src, dst) in enumerate(
            [(state, gs.at[me]), (courant, gc.at[me]), (sections, cs), (fractions, bf), (absorb, idx), (band, bi)]
        )
    ]
    for c in loads:
        c.start()

    def state_copy(d, slot):
        return pltpu.make_async_remote_copy(
            src_ref=gs.at[me], dst_ref=gs.at[slot], send_sem=s_state.at[d], recv_sem=r_state.at[d],
            device_id={"wall": peer(d)}, device_id_type=MESH)

    def line_copy(d, slot):
        return pltpu.make_async_remote_copy(
            src_ref=gc.at[me], dst_ref=gc.at[slot], send_sem=s_cour.at[d], recv_sem=r_cour.at[d],
            device_id={"wall": peer(d)}, device_id_type=MESH)

    def edge_copy(i, d, slot):
        src, dst = ((edge_r, gl), (edge_l, gr))[i]
        return pltpu.make_async_remote_copy(
            src_ref=src, dst_ref=dst.at[slot], send_sem=s_edge.at[i, d], recv_sem=r_edge.at[i, d],
            device_id={"wall": peer(d), "azim": sides[i]}, device_id_type=MESH)

    def edge_copies(d, slot):
        return [edge_copy(i, d, slot) for i in range(2)]

    def send_first(i, _):
        z = peer(i + 1)

        @pl.when((z < me) & (z == 0))
        def _earliest():
            line_copy(i + 1, me).start()
            for c in edge_copies(i + 1, me):
                c.start()
            state_copy(i + 1, me).start()

        return 0

    def say_ready(i, _):
        z = peer(i + 1)

        @pl.when(z < me)
        def _earlier():
            pl.semaphore_signal(ready.at[0, me], inc=1, device_id={"wall": z}, device_id_type=MESH)
            for k, side in enumerate(sides):
                pl.semaphore_signal(ready.at[2 - k, me], inc=1, device_id={"wall": z, "azim": side}, device_id_type=MESH)

        return 0

    def rest_back(i, _):
        z = peer(i + 1)

        @pl.when((z < me) & (z > 0))
        def _earlier():
            state_copy(i + 1, me).start()

        return 0

    def edges_back(i, _):
        z = peer(i + 1)

        @pl.when((z < me) & (z > 0))
        def _earlier():
            @pl.when(z == 1)
            def _paced():
                state_copy(i, me).wait_send()

            line_copy(i + 1, me).start()
            for c in edge_copies(i + 1, me):
                c.start()

        return 0

    def send_on(i, _):
        z = peer(i + 1)

        @pl.when(z > me)
        def _later():
            pl.semaphore_wait(ready.at[0, z], 1)
            line_copy(i + 1, me).start()
            state_copy(i + 1, me).start()
            for k in range(2):
                pl.semaphore_wait(ready.at[1 + k, z], 1)
                edge_copy(k, i + 1, me).start()

        return 0

    for c in loads[:2]:
        c.wait()
    lane = lax.broadcasted_iota(jnp.int32, (rows, lanes), 1)
    el = jnp.zeros((rows, lanes), f32)
    er = jnp.zeros((rows, lanes), f32)
    for c in range(comps + 1):
        x = gs[me, c] if c < comps else gc[me]
        here = (lane >= REACH * c) & (lane < REACH * (c + 1))
        el = jnp.where(here, pltpu.roll(x, REACH * c, 1) if c else x, el)
        er = jnp.where(here, pltpu.roll(x, (REACH * (c + 1)) % lanes, 1), er)
    edge_l[...] = el
    edge_r[...] = er
    greeters = 3 * me + first[0].astype(jnp.int32) + first[1].astype(jnp.int32)

    @pl.when(greeters > 0)
    def _greeted():
        pl.semaphore_wait(barrier, greeters)

    loop(walls - 1, send_first, 0)
    loop(walls - 1, say_ready, 0)
    for i in range(2):

        @pl.when(first[i])
        def _earlier():
            pl.semaphore_signal(ready.at[2 - i, me], inc=1, device_id={"azim": sides[i]}, device_id_type=MESH)

    for i in range(2):

        @pl.when(first[i])
        def _earlier():
            edge_copy(i, 0, me).start()


    for c in loads[2:]:
        c.wait()
    index = idx[...]
    picked = lax.fori_loop(
        0, entries, lambda t, acc: jnp.where(index == t, cs[t], acc), jnp.zeros((species, bands), f32), unroll=8)
    table[...] = jnp.zeros_like(table)
    table[0:species, 0:bands] = picked
    one_hot = jnp.where(
        lax.broadcasted_iota(jnp.int32, (bands, lanes), 0) == lax.broadcasted_iota(jnp.int32, (bands, lanes), 1), 1.0, 0.0)
    by_band = lax.dot_general(one_hot, table[...], (((1,), (1,)), ((), ())), precision=EXACT, preferred_element_type=f32)
    by_band = by_band * (1.0 / total)
    for k in range(species):
        col[k] = jnp.broadcast_to(by_band[:, k : k + 1], (bands, lanes))
    band_row = lax.broadcasted_iota(jnp.int32, (bands, lanes), 0)
    share = jnp.zeros((bands, lanes), f32)
    for b in range(bands):
        share = jnp.where(band_row == b, bf[bi[b]], share)
    share = share * WEIGHTS[0]
    heat_scale = COUPLING * total / 2.0

    def fill(z, values, to_em, to_1, to_2, hot):
        if hot:
            t = fourth(values[0])
        for r in range(rows):
            part = slice(r * bands, (r + 1) * bands)
            step = col[0] * values[1][r : r + 1]
            for k in range(1, species):
                step = step + col[k] * values[1 + k][r : r + 1]
            to_1[z, part] = jnp.exp(step * (-0.5 * RATES[0]))
            to_2[z, part] = jnp.exp(step * (-0.5 * RATES[1]))
            to_em[z, part] = step * (share * t[r : r + 1] if hot else share)

    def fourth(t):
        t = t * t
        return t * t

    def fold(a):
        s = a[0:8]
        for k in range(8, bands, 8):
            s = s + a[k : k + 8]
        return s

    def scan(sets):
        zero = jnp.zeros((bands, lanes), f32)
        ratio = WEIGHTS[1] / WEIGHTS[0]
        n = len(sets)

        def up(z, carry):
            carry = list(carry)
            for r in range(rows):
                part = slice(r * bands, (r + 1) * bands)
                for i, (src, a, b, out) in enumerate(sets):
                    u1, u2, a1, a2 = carry[i]
                    e, b1, b2 = src[z, part], a[z, part], b[z, part]
                    u1 = e + (a1 * b1) * u1
                    u2 = ratio * e + (a2 * b2) * u2
                    out[1 + z * rows + r] = fold(u1 + u2)
                    carry[i] = (u1, u2, b1, b2)
            return tuple(carry)

        def down(k, carry):
            carry = list(carry)
            z = walls - 1 - k
            for r in reversed(range(rows)):
                part = slice(r * bands, (r + 1) * bands)
                for i, (src, a, b, out) in enumerate(sets):
                    d1, d2, a1, a2 = carry[i]
                    e, b1, b2 = src[z, part], a[z, part], b[z, part]
                    d1 = e + (a1 * b1) * d1
                    d2 = ratio * e + (a2 * b2) * d2
                    at = 1 + z * rows + r
                    out[at] = out[at] - fold(d1 + d2)
                    carry[i] = (d1, d2, b1, b2)
            return tuple(carry)

        start = ((zero,) * 4,) * n
        loop(walls, up, start)
        ends = loop(walls, down, start)
        for _s, _a, _b, out in sets:
            out[0] = out[1]
            out[total + 1] = out[total]
        d1, d2, a1, a2 = ends[0]
        return jnp.sum(fold(a1 * d1 + a2 * d2), axis=0, keepdims=True)

    sub = lax.broadcasted_iota(jnp.int32, (rows, lanes), 0)

    def heat(ref, z):
        at = z * rows
        a = [ref[at + i] - ref[at + i + 2] for i in range(rows)]
        order = [4 * ((s >> 2) & 1) + 2 * (1 - ((s >> 1) & 1)) + (1 - (s & 1)) for s in range(8)]
        a = [a[order.index(i)] for i in range(8)]
        low = sub < 4
        b = [jnp.where(low, a[i], a[i + 4]) + pltpu.roll(jnp.where(low, a[i + 4], a[i]), 4, 0) for i in range(4)]
        low = (sub & 3) < 2
        c = [
            jnp.where(low, b[i + 2] + pltpu.roll(b[i + 2], rows - 2, 0), b[i] + pltpu.roll(b[i], 2, 0))
            for i in range(2)
        ]
        low = (sub & 1) < 1
        d = jnp.where(low, c[1] + pltpu.roll(c[1], rows - 1, 0), c[0] + pltpu.roll(c[0], 1, 0))
        return heat_scale * d

    def around(x, h):
        s = {0: x}
        for o in (1, 2, 3):
            s[o] = pltpu.roll(jnp.where(lane >= o, x, h), lanes - o, 1)
            s[-o] = pltpu.roll(jnp.where(lane < lanes - o, x, h), o, 1)
        return s

    def tendency(s, cour):
        gradient = (45.0 / 60.0) * (s[1] - s[-1]) - (9.0 / 60.0) * (s[2] - s[-2]) + (1.0 / 60.0) * (s[3] - s[-3])
        smooth = (s[-3] + s[3]) - 6.0 * (s[-2] + s[2]) + 15.0 * (s[-1] + s[1]) - 20.0 * s[0]
        return FILTER * smooth - cour * gradient

    left_half = lane < lanes // 2

    def halo_of(pr, pk, c):
        a = pltpu.roll(pr, lanes - REACH * c, 1) if c else pr
        return jnp.where(left_half, a, pltpu.roll(pk, lanes - REACH * (c + 1), 1))

    def block(z):
        x = gs[z]
        fill(z, x, em, t1, t2, True)
        pr, pk = gr[z], gl[z]
        h = [halo_of(pr, pk, c) for c in range(comps)]
        fill(z, h, em_h, t1_h, t2_h, True)
        cour = gc[z]
        m = [x[c] + tendency(around(x[c], h[c]), cour) for c in range(comps)]
        for c in range(comps):
            ms[z, c] = m[c]
        fill(z, m, em_m, t1_m, t2_m, False)

    for i in range(2):

        @pl.when(jnp.logical_not(first[i]))
        def _later():
            pl.semaphore_wait(ready.at[1 + i, me], 1)
            edge_copy(i, 0, me).start()

    loop(walls - 1, send_on, 0)
    loop(walls - 1, edges_back, 0)
    loop(walls - 1, rest_back, 0)
    for c in edge_copies(0, me):
        c.wait_recv()
    block(me)
    pr, pk = gr[me], gl[me]
    hc = halo_of(pr, pk, comps)
    cour = gc[me]
    for c in range(comps):
        h = halo_of(pr, pk, c)
        x = gs[me, c]
        mh[c] = h + tendency(around(h, x), hc)
        if c:
            m = ms[me, c]
            new_state[c] = 0.5 * (x + m + tendency(around(m, mh[c]), cour))

    def arrive(i, _):
        z = peer(i + 1)
        d = walls - 1 - i
        state_copy(d, z).wait_recv()
        line_copy(d, z).wait_recv()
        for c in edge_copies(d, z):
            c.wait_recv()
        block(z)
        return 0

    lax.fori_loop(0, walls - 1, arrive, 0)
    flux = scan([(em, t1, t2, net), (em_h, t1_h, t2_h, net_h)])

    def middle(z, _):
        m = ms[z, 0] + heat(net, z)
        ms[z, 0] = m
        t = fourth(m)
        for r in range(rows):
            part = slice(r * bands, (r + 1) * bands)
            em_m[z, part] = em_m[z, part] * t[r : r + 1]
        return 0

    loop(walls, middle, 0)
    flux = flux + scan([(em_m, t1_m, t2_m, net)])
    wall_out[...] = 0.5 * flux
    m = ms[me, 0]
    h = mh[0] + heat(net_h, me)
    new_state[0] = 0.5 * (gs[me, 0] + m + tendency(around(m, h), cour) + heat(net, me))

    def finish(i, _):
        nxt = peer(i + 2)

        @pl.when(jnp.logical_not((nxt < me) & (nxt == 1)))
        def _last():
            state_copy(i + 1, me).wait_send()

        line_copy(i + 1, me).wait_send()
        for c in edge_copies(i + 1, me):
            c.wait_send()
        return 0

    loop(walls - 1, finish, 0)
    for c in edge_copies(0, me):
        c.wait_send()


def hand_over(a, b, a_out, b_out, sems):
    copies = [pltpu.make_async_copy(a, a_out, sems.at[0]), pltpu.make_async_copy(b, b_out, sems.at[1])]
    for c in copies:
        c.start()
    for c in copies:
        c.wait()


def local(walls, azims, state, courant, cross_sections, band_fractions, absorb_index, band_index):
    comps, stations, rows, lanes = state.shape
    bands = absorb_index.shape[1]
    species = absorb_index.shape[0]
    entries = cross_sections.shape[0]
    total = rows * walls
    f32 = jnp.float32
    vmem = pltpu.VMEM
    dma = pltpu.SemaphoreType.DMA
    hbm_spec = pl.BlockSpec(memory_space=pltpu.HBM)
    vmem_spec = pl.BlockSpec(memory_space=pltpu.VMEM)
    new_state, wall = pl.pallas_call(
        functools.partial(kernel, walls, azims),
        out_shape=(
            pltpu.VMEM((comps, rows, lanes), f32),
            pltpu.VMEM((1, lanes), f32),
        ),
        in_specs=[hbm_spec] * 6,
        out_specs=(vmem_spec, vmem_spec),
        scratch_shapes=[
            vmem((walls, comps, rows, lanes), f32),
            vmem((walls, rows, lanes), f32),
            vmem((walls, rows, lanes), f32),
            vmem((walls, rows, lanes), f32),
            vmem((walls, comps, rows, lanes), f32),
            vmem((comps, rows, lanes), f32),
            vmem((rows, lanes), f32),
            vmem((rows, lanes), f32),
        ] + [vmem((walls, rows * bands, lanes), f32)] * 9 + [
            vmem((total + 2, 8, lanes), f32),
            vmem((total + 2, 8, lanes), f32),
            vmem((16, lanes), f32),
            vmem((species, bands, lanes), f32),
            vmem((species, bands), jnp.int32),
            pltpu.SMEM((entries,), f32),
            pltpu.SMEM((entries,), f32),
            pltpu.SMEM((bands,), jnp.int32),
            dma((6,)),
        ] + [dma((walls,))] * 4 + [dma((2, walls))] * 2 + [pltpu.SemaphoreType.REGULAR((3, walls))],
        compiler_params=pltpu.CompilerParams(
            collective_id=0, has_side_effects=True, vmem_limit_bytes=58 * 1024 * 1024),
    )(state.reshape(comps, rows, lanes), courant.reshape(rows, lanes), cross_sections, band_fractions, absorb_index, band_index)
    hbm = pl.BlockSpec(memory_space=pltpu.HBM)
    new_state, wall = pl.pallas_call(
        hand_over,
        out_shape=(
            jax.ShapeDtypeStruct((comps, rows, lanes), f32),
            jax.ShapeDtypeStruct((1, lanes), f32),
        ),
        in_specs=[pl.BlockSpec(memory_space=pl.ANY)] * 2,
        out_specs=(hbm, hbm),
        scratch_shapes=[dma((2,))],
    )(pltpu.with_memory_space_constraint(new_state, pltpu.VMEM), pltpu.with_memory_space_constraint(wall, pltpu.VMEM))
    return new_state.reshape(state.shape), wall


def solution(mesh):
    return jax.shard_map(
        functools.partial(local, mesh.shape["wall"], mesh.shape["azim"]),
        mesh=mesh,
        in_specs=(P(None, "case", "wall", "azim"), P("case", "wall", "azim"), P(), P(), P(), P()),
        out_specs=(P(None, "case", "wall", "azim"), P("case", "azim")),
        check_vma=False,
    )
```

```python
import functools

import jax
import jax.numpy as jnp
from jax import lax
from jax.experimental import pallas as pl
from jax.experimental.pallas import tpu as pltpu
from jax.sharding import PartitionSpec as P

WEIGHTS = (0.55, 0.45)
RATES = (1.15, 3.4)
FILTER = 0.02
COUPLING = 0.1
REACH = 6
NEAR = REACH // 2
MESH = pl.DeviceIdType.MESH
EXACT = lax.Precision.HIGHEST


def loop(count, body, init):
    if count <= 4:
        for i in range(count):
            init = body(i, init)
        return init
    return lax.fori_loop(0, count, body, init)


def kernel(
    walls, azims, state, courant, sections, fractions, absorb, band,
    new_state, wall_out,
    gs, gc, gl, gr, ms, mh, edge_l, edge_r,
    em, t1, t2, em_h, t1_h, t2_h, em_m, t1_m, t2_m, net, net_h,
    table, col, spread, gather, idx, cs, bf, bi,
    local_sem, s_state, r_state, s_cour, r_cour, s_edge, r_edge, ready,
):
    comps, rows, lanes = state.shape
    species, bands = absorb.shape
    entries = sections.shape[0]
    total = rows * walls
    f32, bf16 = jnp.float32, jnp.bfloat16
    me = lax.axis_index("wall")
    az = lax.axis_index("azim")
    right, left = lax.rem(az + 1, azims), lax.rem(az + azims - 1, azims)
    sides = (right, left)
    first = ((az == azims - 1) | (az % 2 == 0), (left % 2 == 1) & (left != azims - 1))

    def peer(d):
        return lax.rem(me + d, walls)

    barrier = pltpu.get_barrier_semaphore()

    def greet(i, _):
        z = peer(i + 1)

        @pl.when(z > me)
        def _later():
            pl.semaphore_signal(barrier, inc=1, device_id={"wall": z}, device_id_type=MESH)
            for side in sides:
                pl.semaphore_signal(barrier, inc=1, device_id={"wall": z, "azim": side}, device_id_type=MESH)

        return 0

    loop(walls - 1, greet, 0)
    for i in range(2):

        @pl.when(jnp.logical_not(first[i]))
        def _later():
            pl.semaphore_signal(barrier, inc=1, device_id={"azim": sides[i]}, device_id_type=MESH)

    loads = [
        pltpu.make_async_copy(src, dst, local_sem.at[i])
        for i, (src, dst) in enumerate(
            [(state, gs.at[me]), (courant, gc.at[me]), (sections, cs), (fractions, bf), (absorb, idx), (band, bi)]
        )
    ]
    for c in loads:
        c.start()

    def state_copy(d, slot):
        return pltpu.make_async_remote_copy(
            src_ref=gs.at[me], dst_ref=gs.at[slot], send_sem=s_state.at[d], recv_sem=r_state.at[d],
            device_id={"wall": peer(d)}, device_id_type=MESH)

    def line_copy(d, slot):
        return pltpu.make_async_remote_copy(
            src_ref=gc.at[me], dst_ref=gc.at[slot], send_sem=s_cour.at[d], recv_sem=r_cour.at[d],
            device_id={"wall": peer(d)}, device_id_type=MESH)

    def edge_copy(i, d, slot):
        src, dst = ((edge_r, gl), (edge_l, gr))[i]
        return pltpu.make_async_remote_copy(
            src_ref=src, dst_ref=dst.at[slot], send_sem=s_edge.at[i, d], recv_sem=r_edge.at[i, d],
            device_id={"wall": peer(d), "azim": sides[i]}, device_id_type=MESH)

    def edge_copies(d, slot):
        return [edge_copy(i, d, slot) for i in range(2)]

    def send_first(i, _):
        z = peer(i + 1)

        @pl.when((z < me) & (z == 0))
        def _earliest():
            line_copy(i + 1, me).start()
            for c in edge_copies(i + 1, me):
                c.start()
            state_copy(i + 1, me).start()

        return 0

    def say_ready(i, _):
        z = peer(i + 1)

        @pl.when(z < me)
        def _earlier():
            pl.semaphore_signal(ready.at[0, me], inc=1, device_id={"wall": z}, device_id_type=MESH)
            for k, side in enumerate(sides):
                pl.semaphore_signal(ready.at[2 - k, me], inc=1, device_id={"wall": z, "azim": side}, device_id_type=MESH)

        return 0

    def rest_back(i, _):
        z = peer(i + 1)

        @pl.when((z < me) & (z > 0))
        def _earlier():
            state_copy(i + 1, me).start()

        return 0

    def edges_back(i, _):
        z = peer(i + 1)

        @pl.when((z < me) & (z > 0))
        def _earlier():
            @pl.when(z == 1)
            def _paced():
                state_copy(i, me).wait_send()

            line_copy(i + 1, me).start()
            for c in edge_copies(i + 1, me):
                c.start()

        return 0

    def send_on(i, _):
        z = peer(i + 1)

        @pl.when(z > me)
        def _later():
            pl.semaphore_wait(ready.at[0, z], 1)
            line_copy(i + 1, me).start()
            state_copy(i + 1, me).start()
            for k in range(2):
                pl.semaphore_wait(ready.at[1 + k, z], 1)
                edge_copy(k, i + 1, me).start()

        return 0

    for c in loads[:2]:
        c.wait()
    lane = lax.broadcasted_iota(jnp.int32, (rows, lanes), 1)
    el = jnp.zeros((rows, lanes), f32)
    er = jnp.zeros((rows, lanes), f32)
    lane_r, lane_l = (lane + NEAR) % lanes, (lane + lanes - NEAR) % lanes
    for c in range(comps + 1):
        x = pltpu.roll(gs[me, c] if c < comps else gc[me], (REACH * c + NEAR) % lanes, 1)
        el = jnp.where((lane_l >= REACH * c) & (lane_l < REACH * (c + 1)), x, el)
        er = jnp.where((lane_r >= REACH * c) & (lane_r < REACH * (c + 1)), x, er)
    edge_l[...] = el
    edge_r[...] = er
    greeters = 3 * me + first[0].astype(jnp.int32) + first[1].astype(jnp.int32)

    @pl.when(greeters > 0)
    def _greeted():
        pl.semaphore_wait(barrier, greeters)

    loop(walls - 1, send_first, 0)
    loop(walls - 1, say_ready, 0)
    for i in range(2):

        @pl.when(first[i])
        def _earlier():
            pl.semaphore_signal(ready.at[2 - i, me], inc=1, device_id={"azim": sides[i]}, device_id_type=MESH)

    for i in range(2):

        @pl.when(first[i])
        def _earlier():
            edge_copy(i, 0, me).start()


    for c in loads[2:]:
        c.wait()
    index = idx[...]
    picked = lax.fori_loop(
        0, entries, lambda t, acc: jnp.where(index == t, cs[t], acc), jnp.zeros((species, bands), f32), unroll=8)
    table[...] = jnp.zeros_like(table)
    table[0:species, 0:bands] = picked
    one_hot = jnp.where(
        lax.broadcasted_iota(jnp.int32, (bands, lanes), 0) == lax.broadcasted_iota(jnp.int32, (bands, lanes), 1), 1.0, 0.0)
    by_band = lax.dot_general(one_hot, table[...], (((1,), (1,)), ((), ())), precision=EXACT, preferred_element_type=f32)
    by_band = by_band * (1.0 / total)
    for k in range(species):
        col[k] = jnp.broadcast_to(by_band[:, k : k + 1], (bands, lanes))
    band_row = lax.broadcasted_iota(jnp.int32, (bands, lanes), 0)
    share = jnp.zeros((bands, lanes), f32)
    for b in range(bands):
        share = jnp.where(band_row == b, bf[bi[b]], share)
    share = share * WEIGHTS[0]
    heat_scale = COUPLING * total / 2.0
    share_h = jnp.zeros((rows, lanes), f32)
    for b in range(bands):
        share_h = jnp.where(lane // REACH == b, bf[bi[b]], share_h)
    share_h = share_h * WEIGHTS[0]
    here = lax.broadcasted_iota(jnp.int32, (lanes, lanes), 0)
    there = lax.broadcasted_iota(jnp.int32, (lanes, lanes), 1)
    kpad = table.shape[0]
    by_entry = jnp.where(
        lax.broadcasted_iota(jnp.int32, (lanes, kpad), 0) // REACH == lax.broadcasted_iota(jnp.int32, (lanes, kpad), 1) + 1, 1.0, 0.0)
    by_place = jnp.dot(by_entry, table[...], precision=EXACT, preferred_element_type=f32)
    to_place = jnp.where(here == there // REACH, 1.0, 0.0)
    area = jnp.dot(by_place, to_place, precision=EXACT, preferred_element_type=f32)
    same = here % REACH == there % REACH
    area = jnp.where(same, area, 0.0) * (1.0 / total)
    area_high = area.astype(bf16)
    spread[:, 0:lanes] = area_high
    spread[:, lanes : 2 * lanes] = (area - area_high.astype(f32)).astype(bf16)
    spread[:, 2 * lanes : 3 * lanes] = jnp.where(same & (here < REACH), 1.0, 0.0).astype(bf16)
    gather[...] = jnp.where((here < REACH * bands) & (here % REACH == (there + NEAR) % lanes), 1.0, 0.0).astype(bf16)

    def fill(z, values, to_em, to_1, to_2, hot):
        if hot:
            t = fourth(values[0])
        for r in range(rows):
            part = slice(r * bands, (r + 1) * bands)
            step = col[0] * values[1][r : r + 1]
            for k in range(1, species):
                step = step + col[k] * values[1 + k][r : r + 1]
            to_1[z, part] = jnp.exp(step * (-0.5 * RATES[0]))
            to_2[z, part] = jnp.exp(step * (-0.5 * RATES[1]))
            to_em[z, part] = step * (share * t[r : r + 1] if hot else share)

    def fourth(t):
        t = t * t
        return t * t

    def fold(a):
        s = a[0:8]
        for k in range(8, bands, 8):
            s = s + a[k : k + 8]
        return s

    ratio = WEIGHTS[1] / WEIGHTS[0]

    def scan(src, a, b):
        zero = jnp.zeros((bands, lanes), f32)

        def up(z, carry):
            u1, u2, a1, a2 = carry
            for r in range(rows):
                part = slice(r * bands, (r + 1) * bands)
                e, b1, b2 = src[z, part], a[z, part], b[z, part]
                u1 = e + (a1 * b1) * u1
                u2 = ratio * e + (a2 * b2) * u2
                net[1 + z * rows + r] = fold(u1 + u2)
                a1, a2 = b1, b2
            return u1, u2, a1, a2

        def down(k, carry):
            d1, d2, a1, a2 = carry
            z = walls - 1 - k
            for r in reversed(range(rows)):
                part = slice(r * bands, (r + 1) * bands)
                e, b1, b2 = src[z, part], a[z, part], b[z, part]
                d1 = e + (a1 * b1) * d1
                d2 = ratio * e + (a2 * b2) * d2
                at = 1 + z * rows + r
                net[at] = net[at] - fold(d1 + d2)
                a1, a2 = b1, b2
            return d1, d2, a1, a2

        loop(walls, up, (zero,) * 4)
        d1, d2, a1, a2 = loop(walls, down, (zero,) * 4)
        net[0] = net[1]
        net[total + 1] = net[total]
        return jnp.sum(fold(a1 * d1 + a2 * d2), axis=0, keepdims=True)

    def halves(a):
        high = a.astype(bf16).astype(f32)
        return jnp.concatenate([high, a - high], axis=0).astype(bf16)

    def fill_edge(z, edge):
        out = jnp.dot(halves(edge), spread[...], preferred_element_type=f32)
        step = out[:rows, :lanes] + out[rows:, :lanes] + out[:rows, lanes : 2 * lanes]
        t = fourth(out[:rows, 2 * lanes :] + out[rows:, 2 * lanes :])
        t1_h[z] = jnp.exp(step * (-0.5 * RATES[0]))
        t2_h[z] = jnp.exp(step * (-0.5 * RATES[1]))
        em_h[z] = step * (share_h * t)

    def edge_flux():
        zero = jnp.zeros((1, lanes), f32)

        def line(z, r):
            return em_h[z, r : r + 1], t1_h[z, r : r + 1], t2_h[z, r : r + 1]

        def up(z, carry):
            u1, u2, a1, a2 = carry
            for r in range(rows):
                e, b1, b2 = line(z, r)
                u1 = e + (a1 * b1) * u1
                u2 = ratio * e + (a2 * b2) * u2
                net_h[1 + z * rows + r] = u1 + u2
                a1, a2 = b1, b2
            return u1, u2, a1, a2

        def down(k, carry):
            d1, d2, a1, a2 = carry
            z = walls - 1 - k
            for r in reversed(range(rows)):
                e, b1, b2 = line(z, r)
                d1 = e + (a1 * b1) * d1
                d2 = ratio * e + (a2 * b2) * d2
                at = 1 + z * rows + r
                net_h[at] = net_h[at] - (d1 + d2)
                a1, a2 = b1, b2
            return d1, d2, a1, a2

        loop(walls, up, (zero,) * 4)
        loop(walls, down, (zero,) * 4)
        net_h[0] = net_h[1]
        net_h[total + 1] = net_h[total]

    def edge_heat():
        at = me * rows
        change = jnp.concatenate([net_h[at + i] - net_h[at + i + 2] for i in range(rows)], axis=0)
        out = jnp.dot(halves(change), gather[...], preferred_element_type=f32)
        return heat_scale * (out[:rows] + out[rows:])

    sub = lax.broadcasted_iota(jnp.int32, (rows, lanes), 0)

    def heat(ref, z):
        at = z * rows
        return row_sums([ref[at + i] - ref[at + i + 2] for i in range(rows)])

    def row_sums(a):
        order = [4 * ((s >> 2) & 1) + 2 * (1 - ((s >> 1) & 1)) + (1 - (s & 1)) for s in range(8)]
        a = [a[order.index(i)] for i in range(8)]
        low = sub < 4
        b = [jnp.where(low, a[i], a[i + 4]) + pltpu.roll(jnp.where(low, a[i + 4], a[i]), 4, 0) for i in range(4)]
        low = (sub & 3) < 2
        c = [
            jnp.where(low, b[i + 2] + pltpu.roll(b[i + 2], rows - 2, 0), b[i] + pltpu.roll(b[i], 2, 0))
            for i in range(2)
        ]
        low = (sub & 1) < 1
        d = jnp.where(low, c[1] + pltpu.roll(c[1], rows - 1, 0), c[0] + pltpu.roll(c[0], 1, 0))
        return heat_scale * d

    def around(x, h):
        s = {0: x}
        for o in (1, 2, 3):
            s[o] = pltpu.roll(jnp.where(lane >= o, x, h), lanes - o, 1)
            s[-o] = pltpu.roll(jnp.where(lane < lanes - o, x, h), o, 1)
        return s

    def tendency(s, cour):
        gradient = (45.0 / 60.0) * (s[1] - s[-1]) - (9.0 / 60.0) * (s[2] - s[-2]) + (1.0 / 60.0) * (s[3] - s[-3])
        smooth = (s[-3] + s[3]) - 6.0 * (s[-2] + s[2]) + 15.0 * (s[-1] + s[1]) - 20.0 * s[0]
        return FILTER * smooth - cour * gradient

    left_half = lane < lanes // 2
    def back(c):
        return (lanes - REACH * c - NEAR) % lanes

    def halo_of(pr, pk, c):
        return jnp.where(left_half, pltpu.roll(pr, back(c), 1), pltpu.roll(pk, back(c), 1))

    def near_of(z):
        return jnp.where(lane % REACH < NEAR, gl[z], gr[z])

    def block(z):
        x = gs[z]
        fill(z, x, em, t1, t2, True)
        edge = near_of(z)
        h = [pltpu.roll(edge, back(c), 1) for c in range(comps)]
        fill_edge(z, edge)
        cour = gc[z]
        m = [x[c] + tendency(around(x[c], h[c]), cour) for c in range(comps)]
        for c in range(comps):
            ms[z, c] = m[c]
        fill(z, m, em_m, t1_m, t2_m, False)

    for i in range(2):

        @pl.when(jnp.logical_not(first[i]))
        def _later():
            pl.semaphore_wait(ready.at[1 + i, me], 1)
            edge_copy(i, 0, me).start()

    loop(walls - 1, send_on, 0)
    loop(walls - 1, edges_back, 0)
    loop(walls - 1, rest_back, 0)
    for c in edge_copies(0, me):
        c.wait_recv()
    block(me)
    pr, pk = gr[me], gl[me]
    hc = halo_of(pr, pk, comps)
    cour = gc[me]
    for c in range(comps):
        h = halo_of(pr, pk, c)
        x = gs[me, c]
        mh[c] = h + tendency(around(h, x), hc)
        if c:
            m = ms[me, c]
            new_state[c] = 0.5 * (x + m + tendency(around(m, mh[c]), cour))

    def turn(i):
        if walls != 4:
            return peer(i + 1)
        turns = jnp.where(me == 0, 39, jnp.where(me == 1, 44, jnp.where(me == 2, 28, 18)))
        return (turns >> (2 * i)) & 3

    def arrive(i, _):
        z = turn(i)
        d = lax.rem(me - z + walls, walls)
        state_copy(d, z).wait_recv()
        line_copy(d, z).wait_recv()
        for c in edge_copies(d, z):
            c.wait_recv()
        block(z)
        return 0

    lax.fori_loop(0, walls - 1, arrive, 0)
    flux = scan(em, t1, t2)
    edge_flux()

    def middle(z, _):
        m = ms[z, 0] + heat(net, z)
        ms[z, 0] = m
        t = fourth(m)
        for r in range(rows):
            part = slice(r * bands, (r + 1) * bands)
            em_m[z, part] = em_m[z, part] * t[r : r + 1]
        return 0

    loop(walls, middle, 0)
    flux = flux + scan(em_m, t1_m, t2_m)
    wall_out[...] = 0.5 * flux
    m = ms[me, 0]
    h = mh[0] + edge_heat()
    new_state[0] = 0.5 * (gs[me, 0] + m + tendency(around(m, h), cour) + heat(net, me))

    def finish(i, _):
        nxt = peer(i + 2)

        @pl.when(jnp.logical_not((nxt < me) & (nxt == 1)))
        def _last():
            state_copy(i + 1, me).wait_send()

        line_copy(i + 1, me).wait_send()
        for c in edge_copies(i + 1, me):
            c.wait_send()
        return 0

    loop(walls - 1, finish, 0)
    for c in edge_copies(0, me):
        c.wait_send()


def hand_over(a, b, a_out, b_out, sems):
    copies = [pltpu.make_async_copy(a, a_out, sems.at[0]), pltpu.make_async_copy(b, b_out, sems.at[1])]
    for c in copies:
        c.start()
    for c in copies:
        c.wait()


def local(walls, azims, state, courant, cross_sections, band_fractions, absorb_index, band_index):
    comps, stations, rows, lanes = state.shape
    bands = absorb_index.shape[1]
    species = absorb_index.shape[0]
    entries = cross_sections.shape[0]
    total = rows * walls
    f32 = jnp.float32
    vmem = pltpu.VMEM
    dma = pltpu.SemaphoreType.DMA
    hbm_spec = pl.BlockSpec(memory_space=pltpu.HBM)
    vmem_spec = pl.BlockSpec(memory_space=pltpu.VMEM)
    new_state, wall = pl.pallas_call(
        functools.partial(kernel, walls, azims),
        out_shape=(
            pltpu.VMEM((comps, rows, lanes), f32),
            pltpu.VMEM((1, lanes), f32),
        ),
        in_specs=[hbm_spec] * 6,
        out_specs=(vmem_spec, vmem_spec),
        scratch_shapes=[
            vmem((walls, comps, rows, lanes), f32),
            vmem((walls, rows, lanes), f32),
            vmem((walls, rows, lanes), f32),
            vmem((walls, rows, lanes), f32),
            vmem((walls, comps, rows, lanes), f32),
            vmem((comps, rows, lanes), f32),
            vmem((rows, lanes), f32),
            vmem((rows, lanes), f32),
        ] + [vmem((walls, rows * bands, lanes), f32)] * 3 + [vmem((walls, rows, lanes), f32)] * 3 + [
            vmem((walls, rows * bands, lanes), f32)] * 3 + [
            vmem((total + 2, 8, lanes), f32),
            vmem((total + 2, 1, lanes), f32),
            vmem((16, lanes), f32),
            vmem((species, bands, lanes), f32),
            vmem((lanes, 3 * lanes), jnp.bfloat16),
            vmem((lanes, lanes), jnp.bfloat16),
            vmem((species, bands), jnp.int32),
            pltpu.SMEM((entries,), f32),
            pltpu.SMEM((entries,), f32),
            pltpu.SMEM((bands,), jnp.int32),
            dma((6,)),
        ] + [dma((walls,))] * 4 + [dma((2, walls))] * 2 + [pltpu.SemaphoreType.REGULAR((3, walls))],
        compiler_params=pltpu.CompilerParams(
            collective_id=0, has_side_effects=True, vmem_limit_bytes=58 * 1024 * 1024),
    )(state.reshape(comps, rows, lanes), courant.reshape(rows, lanes), cross_sections, band_fractions, absorb_index, band_index)
    hbm = pl.BlockSpec(memory_space=pltpu.HBM)
    new_state, wall = pl.pallas_call(
        hand_over,
        out_shape=(
            jax.ShapeDtypeStruct((comps, rows, lanes), f32),
            jax.ShapeDtypeStruct((1, lanes), f32),
        ),
        in_specs=[pl.BlockSpec(memory_space=pl.ANY)] * 2,
        out_specs=(hbm, hbm),
        scratch_shapes=[dma((2,))],
    )(pltpu.with_memory_space_constraint(new_state, pltpu.VMEM), pltpu.with_memory_space_constraint(wall, pltpu.VMEM))
    return new_state.reshape(state.shape), wall


def solution(mesh):
    return jax.shard_map(
        functools.partial(local, mesh.shape["wall"], mesh.shape["azim"]),
        mesh=mesh,
        in_specs=(P(None, "case", "wall", "azim"), P("case", "wall", "azim"), P(), P(), P(), P()),
        out_specs=(P(None, "case", "wall", "azim"), P("case", "azim")),
        check_vma=False,
    )
```

```python
import functools

import jax
import jax.numpy as jnp
from jax import lax
from jax.experimental import pallas as pl
from jax.experimental.pallas import tpu as pltpu
from jax.sharding import PartitionSpec as P

WEIGHTS = (0.55, 0.45)
RATES = (1.15, 3.4)
FILTER = 0.02
COUPLING = 0.1
REACH = 6
NEAR = REACH // 2
MESH = pl.DeviceIdType.MESH
EXACT = lax.Precision.HIGHEST


def loop(count, body, init):
    if count <= 4:
        for i in range(count):
            init = body(i, init)
        return init
    return lax.fori_loop(0, count, body, init)


def kernel(
    walls, azims, state, courant, sections, fractions, absorb, band,
    new_state, wall_out,
    gs, gc, gl, gr, ms, mh, edge_l, edge_r,
    em, t1, t2, em_h, t1_h, t2_h, em_m, t1_m, t2_m, net, net_h,
    table, col, spread, gather, idx, cs, bf, bi,
    local_sem, s_state, r_state, s_cour, r_cour, s_edge, r_edge, ready,
):
    comps, rows, lanes = state.shape
    species, bands = absorb.shape
    entries = sections.shape[0]
    total = rows * walls
    f32, bf16 = jnp.float32, jnp.bfloat16
    me = lax.axis_index("wall")
    az = lax.axis_index("azim")
    right, left = lax.rem(az + 1, azims), lax.rem(az + azims - 1, azims)
    sides = (right, left)
    first = ((az == azims - 1) | (az % 2 == 0), (left % 2 == 1) & (left != azims - 1))

    def peer(d):
        return lax.rem(me + d, walls)

    barrier = pltpu.get_barrier_semaphore()

    def greet(i, _):
        z = peer(i + 1)

        @pl.when(z > me)
        def _later():
            pl.semaphore_signal(barrier, inc=1, device_id={"wall": z}, device_id_type=MESH)
            for side in sides:
                pl.semaphore_signal(barrier, inc=1, device_id={"wall": z, "azim": side}, device_id_type=MESH)

        return 0

    loop(walls - 1, greet, 0)
    for i in range(2):

        @pl.when(jnp.logical_not(first[i]))
        def _later():
            pl.semaphore_signal(barrier, inc=1, device_id={"azim": sides[i]}, device_id_type=MESH)

    loads = [
        pltpu.make_async_copy(src, dst, local_sem.at[i])
        for i, (src, dst) in enumerate(
            [(state, gs.at[me]), (courant, gc.at[me]), (sections, cs), (fractions, bf), (absorb, idx), (band, bi)]
        )
    ]
    for c in loads:
        c.start()

    def state_copy(d, slot):
        return pltpu.make_async_remote_copy(
            src_ref=gs.at[me], dst_ref=gs.at[slot], send_sem=s_state.at[d], recv_sem=r_state.at[d],
            device_id={"wall": peer(d)}, device_id_type=MESH)

    def line_copy(d, slot):
        return pltpu.make_async_remote_copy(
            src_ref=gc.at[me], dst_ref=gc.at[slot], send_sem=s_cour.at[d], recv_sem=r_cour.at[d],
            device_id={"wall": peer(d)}, device_id_type=MESH)

    def edge_copy(i, d, slot):
        src, dst = ((edge_r, gl), (edge_l, gr))[i]
        return pltpu.make_async_remote_copy(
            src_ref=src, dst_ref=dst.at[slot], send_sem=s_edge.at[i, d], recv_sem=r_edge.at[i, d],
            device_id={"wall": peer(d), "azim": sides[i]}, device_id_type=MESH)

    def edge_copies(d, slot):
        return [edge_copy(i, d, slot) for i in range(2)]

    def send_first(i, _):
        z = peer(i + 1)

        @pl.when((z < me) & (z == 0))
        def _earliest():
            line_copy(i + 1, me).start()
            for c in edge_copies(i + 1, me):
                c.start()
            state_copy(i + 1, me).start()

        return 0

    def say_ready(i, _):
        z = peer(i + 1)

        @pl.when(z < me)
        def _earlier():
            pl.semaphore_signal(ready.at[0, me], inc=1, device_id={"wall": z}, device_id_type=MESH)
            for k, side in enumerate(sides):
                pl.semaphore_signal(ready.at[2 - k, me], inc=1, device_id={"wall": z, "azim": side}, device_id_type=MESH)

        return 0

    def rest_back(i, _):
        z = peer(i + 1)

        @pl.when((z < me) & (z > 0))
        def _earlier():
            state_copy(i + 1, me).start()

        return 0

    def edges_back(i, _):
        z = peer(i + 1)

        @pl.when((z < me) & (z > 0))
        def _earlier():
            @pl.when(z == 1)
            def _paced():
                state_copy(i, me).wait_send()

            line_copy(i + 1, me).start()
            for c in edge_copies(i + 1, me):
                c.start()

        return 0

    def send_on(i, _):
        z = peer(i + 1)

        @pl.when(z > me)
        def _later():
            pl.semaphore_wait(ready.at[0, z], 1)
            line_copy(i + 1, me).start()

            @pl.when(z < walls - 1)
            def _state():
                state_copy(i + 1, me).start()

            for k in range(2):
                pl.semaphore_wait(ready.at[1 + k, z], 1)
                edge_copy(k, i + 1, me).start()

            @pl.when(z == walls - 1)
            def _last():
                state_copy(i + 1, me).start()

        return 0

    for c in loads[:2]:
        c.wait()
    lane = lax.broadcasted_iota(jnp.int32, (rows, lanes), 1)
    el = jnp.zeros((rows, lanes), f32)
    er = jnp.zeros((rows, lanes), f32)
    lane_r, lane_l = (lane + NEAR) % lanes, (lane + lanes - NEAR) % lanes
    for c in range(comps + 1):
        x = pltpu.roll(gs[me, c] if c < comps else gc[me], (REACH * c + NEAR) % lanes, 1)
        el = jnp.where((lane_l >= REACH * c) & (lane_l < REACH * (c + 1)), x, el)
        er = jnp.where((lane_r >= REACH * c) & (lane_r < REACH * (c + 1)), x, er)
    edge_l[...] = el
    edge_r[...] = er
    greeters = 3 * me + first[0].astype(jnp.int32) + first[1].astype(jnp.int32)

    @pl.when(greeters > 0)
    def _greeted():
        pl.semaphore_wait(barrier, greeters)

    loop(walls - 1, send_first, 0)
    loop(walls - 1, say_ready, 0)
    for i in range(2):

        @pl.when(first[i])
        def _earlier():
            pl.semaphore_signal(ready.at[2 - i, me], inc=1, device_id={"azim": sides[i]}, device_id_type=MESH)

    for i in range(2):

        @pl.when(first[i])
        def _earlier():
            edge_copy(i, 0, me).start()


    for c in loads[2:]:
        c.wait()
    index = idx[...]
    picked = lax.fori_loop(
        0, entries, lambda t, acc: jnp.where(index == t, cs[t], acc), jnp.zeros((species, bands), f32), unroll=8)
    table[...] = jnp.zeros_like(table)
    table[0:species, 0:bands] = picked
    one_hot = jnp.where(
        lax.broadcasted_iota(jnp.int32, (bands, lanes), 0) == lax.broadcasted_iota(jnp.int32, (bands, lanes), 1), 1.0, 0.0)
    by_band = lax.dot_general(one_hot, table[...], (((1,), (1,)), ((), ())), precision=EXACT, preferred_element_type=f32)
    by_band = by_band * (1.0 / total)
    for k in range(species):
        col[k] = jnp.broadcast_to(by_band[:, k : k + 1], (bands, lanes))
    band_row = lax.broadcasted_iota(jnp.int32, (bands, lanes), 0)
    share = jnp.zeros((bands, lanes), f32)
    for b in range(bands):
        share = jnp.where(band_row == b, bf[bi[b]], share)
    share = share * WEIGHTS[0]
    heat_scale = COUPLING * total / 2.0
    share_h = jnp.zeros((rows, lanes), f32)
    for b in range(bands):
        share_h = jnp.where(lane // REACH == b, bf[bi[b]], share_h)
    share_h = share_h * WEIGHTS[0]
    here = lax.broadcasted_iota(jnp.int32, (lanes, lanes), 0)
    there = lax.broadcasted_iota(jnp.int32, (lanes, lanes), 1)
    kpad = table.shape[0]
    by_entry = jnp.where(
        lax.broadcasted_iota(jnp.int32, (lanes, kpad), 0) // REACH == lax.broadcasted_iota(jnp.int32, (lanes, kpad), 1) + 1, 1.0, 0.0)
    by_place = jnp.dot(by_entry, table[...], precision=EXACT, preferred_element_type=f32)
    to_place = jnp.where(here == there // REACH, 1.0, 0.0)
    area = jnp.dot(by_place, to_place, precision=EXACT, preferred_element_type=f32)
    same = here % REACH == there % REACH
    area = jnp.where(same, area, 0.0) * (1.0 / total)
    area_high = area.astype(bf16)
    spread[:, 0:lanes] = area_high
    spread[:, lanes : 2 * lanes] = (area - area_high.astype(f32)).astype(bf16)
    spread[:, 2 * lanes : 3 * lanes] = jnp.where(same & (here < REACH), 1.0, 0.0).astype(bf16)
    gather[...] = jnp.where((here < REACH * bands) & (here % REACH == (there + NEAR) % lanes), 1.0, 0.0).astype(bf16)

    def fill(z, values, to_em, to_1, to_2, hot):
        if hot:
            t = fourth(values[0])
        for r in range(rows):
            part = slice(r * bands, (r + 1) * bands)
            step = col[0] * values[1][r : r + 1]
            for k in range(1, species):
                step = step + col[k] * values[1 + k][r : r + 1]
            to_1[z, part] = jnp.exp(step * (-0.5 * RATES[0]))
            to_2[z, part] = jnp.exp(step * (-0.5 * RATES[1]))
            to_em[z, part] = step * (share * t[r : r + 1] if hot else share)

    def fourth(t):
        t = t * t
        return t * t

    def fold(a):
        s = a[0:8]
        for k in range(8, bands, 8):
            s = s + a[k : k + 8]
        return s

    ratio = WEIGHTS[1] / WEIGHTS[0]

    def scan(src, a, b):
        zero = jnp.zeros((bands, lanes), f32)

        def up(z, carry):
            u1, u2, a1, a2 = carry
            for r in range(rows):
                part = slice(r * bands, (r + 1) * bands)
                e, b1, b2 = src[z, part], a[z, part], b[z, part]
                u1 = e + (a1 * b1) * u1
                u2 = ratio * e + (a2 * b2) * u2
                net[1 + z * rows + r] = fold(u1 + u2)
                a1, a2 = b1, b2
            return u1, u2, a1, a2

        def down(k, carry):
            d1, d2, a1, a2 = carry
            z = walls - 1 - k
            for r in reversed(range(rows)):
                part = slice(r * bands, (r + 1) * bands)
                e, b1, b2 = src[z, part], a[z, part], b[z, part]
                d1 = e + (a1 * b1) * d1
                d2 = ratio * e + (a2 * b2) * d2
                at = 1 + z * rows + r
                net[at] = net[at] - fold(d1 + d2)
                a1, a2 = b1, b2
            return d1, d2, a1, a2

        loop(walls, up, (zero,) * 4)
        d1, d2, a1, a2 = loop(walls, down, (zero,) * 4)
        net[0] = net[1]
        net[total + 1] = net[total]
        return jnp.sum(fold(a1 * d1 + a2 * d2), axis=0, keepdims=True)

    def halves(a):
        high = a.astype(bf16).astype(f32)
        return jnp.concatenate([high, a - high], axis=0).astype(bf16)

    def fill_edge(z, edge):
        out = jnp.dot(halves(edge), spread[...], preferred_element_type=f32)
        step = out[:rows, :lanes] + out[rows:, :lanes] + out[:rows, lanes : 2 * lanes]
        t = fourth(out[:rows, 2 * lanes :] + out[rows:, 2 * lanes :])
        t1_h[z] = jnp.exp(step * (-0.5 * RATES[0]))
        t2_h[z] = jnp.exp(step * (-0.5 * RATES[1]))
        em_h[z] = step * (share_h * t)

    def edge_flux():
        zero = jnp.zeros((1, lanes), f32)

        def line(z, r):
            return em_h[z, r : r + 1], t1_h[z, r : r + 1], t2_h[z, r : r + 1]

        def up(z, carry):
            u1, u2, a1, a2 = carry
            for r in range(rows):
                e, b1, b2 = line(z, r)
                u1 = e + (a1 * b1) * u1
                u2 = ratio * e + (a2 * b2) * u2
                net_h[1 + z * rows + r] = u1 + u2
                a1, a2 = b1, b2
            return u1, u2, a1, a2

        def down(k, carry):
            d1, d2, a1, a2 = carry
            z = walls - 1 - k
            for r in reversed(range(rows)):
                e, b1, b2 = line(z, r)
                d1 = e + (a1 * b1) * d1
                d2 = ratio * e + (a2 * b2) * d2
                at = 1 + z * rows + r
                net_h[at] = net_h[at] - (d1 + d2)
                a1, a2 = b1, b2
            return d1, d2, a1, a2

        loop(walls, up, (zero,) * 4)
        loop(walls, down, (zero,) * 4)
        net_h[0] = net_h[1]
        net_h[total + 1] = net_h[total]

    def edge_heat():
        at = me * rows
        change = jnp.concatenate([net_h[at + i] - net_h[at + i + 2] for i in range(rows)], axis=0)
        out = jnp.dot(halves(change), gather[...], preferred_element_type=f32)
        return heat_scale * (out[:rows] + out[rows:])

    sub = lax.broadcasted_iota(jnp.int32, (rows, lanes), 0)

    def heat(ref, z):
        at = z * rows
        return row_sums([ref[at + i] - ref[at + i + 2] for i in range(rows)])

    def row_sums(a):
        order = [4 * ((s >> 2) & 1) + 2 * (1 - ((s >> 1) & 1)) + (1 - (s & 1)) for s in range(8)]
        a = [a[order.index(i)] for i in range(8)]
        low = sub < 4
        b = [jnp.where(low, a[i], a[i + 4]) + pltpu.roll(jnp.where(low, a[i + 4], a[i]), 4, 0) for i in range(4)]
        low = (sub & 3) < 2
        c = [
            jnp.where(low, b[i + 2] + pltpu.roll(b[i + 2], rows - 2, 0), b[i] + pltpu.roll(b[i], 2, 0))
            for i in range(2)
        ]
        low = (sub & 1) < 1
        d = jnp.where(low, c[1] + pltpu.roll(c[1], rows - 1, 0), c[0] + pltpu.roll(c[0], 1, 0))
        return heat_scale * d

    def around(x, h):
        s = {0: x}
        for o in (1, 2, 3):
            s[o] = pltpu.roll(jnp.where(lane >= o, x, h), lanes - o, 1)
            s[-o] = pltpu.roll(jnp.where(lane < lanes - o, x, h), o, 1)
        return s

    def tendency(s, cour):
        gradient = (45.0 / 60.0) * (s[1] - s[-1]) - (9.0 / 60.0) * (s[2] - s[-2]) + (1.0 / 60.0) * (s[3] - s[-3])
        smooth = (s[-3] + s[3]) - 6.0 * (s[-2] + s[2]) + 15.0 * (s[-1] + s[1]) - 20.0 * s[0]
        return FILTER * smooth - cour * gradient

    left_half = lane < lanes // 2
    def back(c):
        return (lanes - REACH * c - NEAR) % lanes

    def halo_of(pr, pk, c):
        return jnp.where(left_half, pltpu.roll(pr, back(c), 1), pltpu.roll(pk, back(c), 1))

    def near_of(z):
        return jnp.where(lane % REACH < NEAR, gl[z], gr[z])

    def block(z):
        x = gs[z]
        fill(z, x, em, t1, t2, True)
        edge = near_of(z)
        h = [pltpu.roll(edge, back(c), 1) for c in range(comps)]
        fill_edge(z, edge)
        cour = gc[z]
        m = [x[c] + tendency(around(x[c], h[c]), cour) for c in range(comps)]
        for c in range(comps):
            ms[z, c] = m[c]
        fill(z, m, em_m, t1_m, t2_m, False)

    for i in range(2):

        @pl.when(jnp.logical_not(first[i]))
        def _later():
            pl.semaphore_wait(ready.at[1 + i, me], 1)
            edge_copy(i, 0, me).start()

    loop(walls - 1, send_on, 0)
    loop(walls - 1, edges_back, 0)
    loop(walls - 1, rest_back, 0)
    def turn(i):
        if walls != 4:
            return peer(i + 1)
        turns = jnp.where(me == 0, 39, jnp.where(me == 1, 44, jnp.where(me == 2, 28, 18)))
        return (turns >> (2 * i)) & 3

    def arrive(i, _):
        z = jnp.where(i == 0, me, turn(jnp.maximum(i - 1, 0)))
        d = lax.rem(me - z + walls, walls)

        @pl.when(i > 0)
        def _other():
            state_copy(d, z).wait_recv()
            line_copy(d, z).wait_recv()

        for c in edge_copies(d, z):
            c.wait_recv()
        block(z)

        @pl.when(i == 0)
        def _own():
            pr, pk = gr[me], gl[me]
            hc = halo_of(pr, pk, comps)
            cour = gc[me]
            for c in range(comps):
                h = halo_of(pr, pk, c)
                x = gs[me, c]
                mh[c] = h + tendency(around(h, x), hc)
                if c:
                    m = ms[me, c]
                    new_state[c] = 0.5 * (x + m + tendency(around(m, mh[c]), cour))

        return 0

    lax.fori_loop(0, walls, arrive, 0)
    edge_flux()
    flux = scan(em, t1, t2)
    heat_h = edge_heat()

    def middle(z, _):
        m = ms[z, 0] + heat(net, z)
        ms[z, 0] = m
        t = fourth(m)
        for r in range(rows):
            part = slice(r * bands, (r + 1) * bands)
            em_m[z, part] = em_m[z, part] * t[r : r + 1]
        return 0

    loop(walls, middle, 0)
    flux = flux + scan(em_m, t1_m, t2_m)
    wall_out[...] = 0.5 * flux
    cour = gc[me]
    m = ms[me, 0]
    h = mh[0] + heat_h
    new_state[0] = 0.5 * (gs[me, 0] + m + tendency(around(m, h), cour) + heat(net, me))

    def finish(i, _):
        nxt = peer(i + 2)

        @pl.when(jnp.logical_not((nxt < me) & (nxt == 1)))
        def _last():
            state_copy(i + 1, me).wait_send()

        line_copy(i + 1, me).wait_send()
        for c in edge_copies(i + 1, me):
            c.wait_send()
        return 0

    loop(walls - 1, finish, 0)
    for c in edge_copies(0, me):
        c.wait_send()


def hand_over(a, b, a_out, b_out, sems):
    copies = [pltpu.make_async_copy(a, a_out, sems.at[0]), pltpu.make_async_copy(b, b_out, sems.at[1])]
    for c in copies:
        c.start()
    for c in copies:
        c.wait()


def local(walls, azims, state, courant, cross_sections, band_fractions, absorb_index, band_index):
    comps, stations, rows, lanes = state.shape
    bands = absorb_index.shape[1]
    species = absorb_index.shape[0]
    entries = cross_sections.shape[0]
    total = rows * walls
    f32 = jnp.float32
    vmem = pltpu.VMEM
    dma = pltpu.SemaphoreType.DMA
    hbm_spec = pl.BlockSpec(memory_space=pltpu.HBM)
    vmem_spec = pl.BlockSpec(memory_space=pltpu.VMEM)
    new_state, wall = pl.pallas_call(
        functools.partial(kernel, walls, azims),
        out_shape=(
            pltpu.VMEM((comps, rows, lanes), f32),
            pltpu.VMEM((1, lanes), f32),
        ),
        in_specs=[hbm_spec] * 6,
        out_specs=(vmem_spec, vmem_spec),
        scratch_shapes=[
            vmem((walls, comps, rows, lanes), f32),
            vmem((walls, rows, lanes), f32),
            vmem((walls, rows, lanes), f32),
            vmem((walls, rows, lanes), f32),
            vmem((walls, comps, rows, lanes), f32),
            vmem((comps, rows, lanes), f32),
            vmem((rows, lanes), f32),
            vmem((rows, lanes), f32),
        ] + [vmem((walls, rows * bands, lanes), f32)] * 3 + [vmem((walls, rows, lanes), f32)] * 3 + [
            vmem((walls, rows * bands, lanes), f32)] * 3 + [
            vmem((total + 2, 8, lanes), f32),
            vmem((total + 2, 1, lanes), f32),
            vmem((16, lanes), f32),
            vmem((species, bands, lanes), f32),
            vmem((lanes, 3 * lanes), jnp.bfloat16),
            vmem((lanes, lanes), jnp.bfloat16),
            vmem((species, bands), jnp.int32),
            pltpu.SMEM((entries,), f32),
            pltpu.SMEM((entries,), f32),
            pltpu.SMEM((bands,), jnp.int32),
            dma((6,)),
        ] + [dma((walls,))] * 4 + [dma((2, walls))] * 2 + [pltpu.SemaphoreType.REGULAR((3, walls))],
        compiler_params=pltpu.CompilerParams(
            collective_id=0, has_side_effects=True, vmem_limit_bytes=58 * 1024 * 1024),
    )(state.reshape(comps, rows, lanes), courant.reshape(rows, lanes), cross_sections, band_fractions, absorb_index, band_index)
    hbm = pl.BlockSpec(memory_space=pltpu.HBM)
    new_state, wall = pl.pallas_call(
        hand_over,
        out_shape=(
            jax.ShapeDtypeStruct((comps, rows, lanes), f32),
            jax.ShapeDtypeStruct((1, lanes), f32),
        ),
        in_specs=[pl.BlockSpec(memory_space=pl.ANY)] * 2,
        out_specs=(hbm, hbm),
        scratch_shapes=[dma((2,))],
    )(pltpu.with_memory_space_constraint(new_state, pltpu.VMEM), pltpu.with_memory_space_constraint(wall, pltpu.VMEM))
    return new_state.reshape(state.shape), wall


def solution(mesh):
    return jax.shard_map(
        functools.partial(local, mesh.shape["wall"], mesh.shape["azim"]),
        mesh=mesh,
        in_specs=(P(None, "case", "wall", "azim"), P("case", "wall", "azim"), P(), P(), P(), P()),
        out_specs=(P(None, "case", "wall", "azim"), P("case", "azim")),
        check_vma=False,
    )
```

```python
import functools

import jax
import jax.numpy as jnp
from jax import lax
from jax.experimental import pallas as pl
from jax.experimental.pallas import tpu as pltpu
from jax.sharding import PartitionSpec as P

WEIGHTS = (0.55, 0.45)
RATES = (1.15, 3.4)
FILTER = 0.02
COUPLING = 0.1
REACH = 6
NEAR = REACH // 2
MESH = pl.DeviceIdType.MESH
EXACT = lax.Precision.HIGHEST


def loop(count, body, init):
    if count <= 4:
        for i in range(count):
            init = body(i, init)
        return init
    return lax.fori_loop(0, count, body, init)


def kernel(
    walls, azims, state, courant, sections, fractions, absorb, band,
    new_state, wall_out,
    gs, gc, gl, gr, ms, mh, edge_l, edge_r,
    em, t1, t2, em_h, t1_h, t2_h, em_m, t1_m, t2_m, first_t, first_m, net, net_h,
    table, col, spread, gather, idx, cs, bf, bi,
    local_sem, s_state, r_state, s_cour, r_cour, s_edge, r_edge, ready,
):
    comps, rows, lanes = state.shape
    species, bands = absorb.shape
    entries = sections.shape[0]
    total = rows * walls
    f32, bf16 = jnp.float32, jnp.bfloat16
    me = lax.axis_index("wall")
    az = lax.axis_index("azim")
    right, left = lax.rem(az + 1, azims), lax.rem(az + azims - 1, azims)
    sides = (right, left)
    first = ((az == azims - 1) | (az % 2 == 0), (left % 2 == 1) & (left != azims - 1))

    def peer(d):
        return lax.rem(me + d, walls)

    barrier = pltpu.get_barrier_semaphore()

    def greet(i, _):
        z = peer(i + 1)

        @pl.when(z > me)
        def _later():
            pl.semaphore_signal(barrier, inc=1, device_id={"wall": z}, device_id_type=MESH)
            for side in sides:
                pl.semaphore_signal(barrier, inc=1, device_id={"wall": z, "azim": side}, device_id_type=MESH)

        return 0

    loop(walls - 1, greet, 0)
    for i in range(2):

        @pl.when(jnp.logical_not(first[i]))
        def _later():
            pl.semaphore_signal(barrier, inc=1, device_id={"azim": sides[i]}, device_id_type=MESH)

    loads = [
        pltpu.make_async_copy(src, dst, local_sem.at[i])
        for i, (src, dst) in enumerate(
            [(state, gs.at[me]), (courant, gc.at[me]), (sections, cs), (fractions, bf), (absorb, idx), (band, bi)]
        )
    ]
    for c in loads:
        c.start()

    def state_copy(d, slot):
        return pltpu.make_async_remote_copy(
            src_ref=gs.at[me], dst_ref=gs.at[slot], send_sem=s_state.at[d], recv_sem=r_state.at[d],
            device_id={"wall": peer(d)}, device_id_type=MESH)

    def line_copy(d, slot):
        return pltpu.make_async_remote_copy(
            src_ref=gc.at[me], dst_ref=gc.at[slot], send_sem=s_cour.at[d], recv_sem=r_cour.at[d],
            device_id={"wall": peer(d)}, device_id_type=MESH)

    def edge_copy(i, d, slot):
        src, dst = ((edge_r, gl), (edge_l, gr))[i]
        return pltpu.make_async_remote_copy(
            src_ref=src, dst_ref=dst.at[slot], send_sem=s_edge.at[i, d], recv_sem=r_edge.at[i, d],
            device_id={"wall": peer(d), "azim": sides[i]}, device_id_type=MESH)

    def edge_copies(d, slot):
        return [edge_copy(i, d, slot) for i in range(2)]

    def send_first(i, _):
        z = peer(i + 1)

        @pl.when((z < me) & (z == 0))
        def _earliest():
            line_copy(i + 1, me).start()
            for c in edge_copies(i + 1, me):
                c.start()

            @pl.when(jnp.logical_not((me == walls - 1) | ((me == 1) & (az % 2 == 1))))
            def _at_once():
                state_copy(i + 1, me).start()

        return 0

    def send_next(i, _):
        z = peer(i + 1)

        @pl.when((z < me) & (z == 0) & (me == walls - 1))
        def _after():
            state_copy(i + 1, me).start()

        return 0

    def send_late(i, _):
        z = peer(i + 1)

        @pl.when((z < me) & (z == 0) & (me < walls - 1) & ((me == 1) & (az % 2 == 1)))
        def _late():
            state_copy(i + 1, me).start()

        return 0

    def say_ready(i, _):
        z = peer(i + 1)

        @pl.when(z < me)
        def _earlier():
            pl.semaphore_signal(ready.at[0, me], inc=1, device_id={"wall": z}, device_id_type=MESH)
            for k, side in enumerate(sides):
                pl.semaphore_signal(ready.at[2 - k, me], inc=1, device_id={"wall": z, "azim": side}, device_id_type=MESH)

        return 0

    def rest_back(i, _):
        z = peer(i + 1)

        @pl.when((z < me) & (z > 0))
        def _earlier():
            state_copy(i + 1, me).start()

        return 0

    def edges_back(i, _):
        z = peer(i + 1)

        @pl.when((z < me) & (z > 0))
        def _earlier():
            @pl.when(z == 1)
            def _paced():
                state_copy(i, me).wait_send()

            line_copy(i + 1, me).start()
            for c in edge_copies(i + 1, me):
                c.start()

        return 0

    def send_on(i, _):
        z = peer(i + 1)

        @pl.when(z > me)
        def _later():
            pl.semaphore_wait(ready.at[0, z], 1)
            line_copy(i + 1, me).start()

            @pl.when(z < walls - 1)
            def _state():
                state_copy(i + 1, me).start()

            for k in range(2):
                pl.semaphore_wait(ready.at[1 + k, z], 1)
                edge_copy(k, i + 1, me).start()

            @pl.when(z == walls - 1)
            def _last():
                state_copy(i + 1, me).start()

        return 0

    for c in loads[:2]:
        c.wait()
    lane = lax.broadcasted_iota(jnp.int32, (rows, lanes), 1)
    el = jnp.zeros((rows, lanes), f32)
    er = jnp.zeros((rows, lanes), f32)
    lane_r, lane_l = (lane + NEAR) % lanes, (lane + lanes - NEAR) % lanes
    for c in range(comps + 1):
        x = pltpu.roll(gs[me, c] if c < comps else gc[me], (REACH * c + NEAR) % lanes, 1)
        el = jnp.where((lane_l >= REACH * c) & (lane_l < REACH * (c + 1)), x, el)
        er = jnp.where((lane_r >= REACH * c) & (lane_r < REACH * (c + 1)), x, er)
    edge_l[...] = el
    edge_r[...] = er
    greeters = 3 * me + first[0].astype(jnp.int32) + first[1].astype(jnp.int32)

    @pl.when(greeters > 0)
    def _greeted():
        pl.semaphore_wait(barrier, greeters)

    loop(walls - 1, send_first, 0)
    loop(walls - 1, say_ready, 0)
    for i in range(2):

        @pl.when(first[i])
        def _earlier():
            pl.semaphore_signal(ready.at[2 - i, me], inc=1, device_id={"azim": sides[i]}, device_id_type=MESH)

    for i in range(2):

        @pl.when(first[i])
        def _earlier():
            edge_copy(i, 0, me).start()


    loop(walls - 1, send_next, 0)
    for c in loads[2:]:
        c.wait()
    index = idx[...]
    picked = lax.fori_loop(
        0, entries, lambda t, acc: jnp.where(index == t, cs[t], acc), jnp.zeros((species, bands), f32), unroll=8)
    table[...] = jnp.zeros_like(table)
    table[0:species, 0:bands] = picked
    one_hot = jnp.where(
        lax.broadcasted_iota(jnp.int32, (bands, lanes), 0) == lax.broadcasted_iota(jnp.int32, (bands, lanes), 1), 1.0, 0.0)
    by_band = lax.dot_general(one_hot, table[...], (((1,), (1,)), ((), ())), precision=EXACT, preferred_element_type=f32)
    by_band = by_band * (1.0 / total)
    for k in range(species):
        col[k] = jnp.broadcast_to(by_band[:, k : k + 1], (bands, lanes))
    band_row = lax.broadcasted_iota(jnp.int32, (bands, lanes), 0)
    share = jnp.zeros((bands, lanes), f32)
    for b in range(bands):
        share = jnp.where(band_row == b, bf[bi[b]], share)
    share = share * WEIGHTS[0]
    heat_scale = COUPLING * total / 2.0
    share_h = jnp.zeros((rows, lanes), f32)
    for b in range(bands):
        share_h = jnp.where(lane // REACH == b, bf[bi[b]], share_h)
    share_h = share_h * WEIGHTS[0]
    here = lax.broadcasted_iota(jnp.int32, (lanes, lanes), 0)
    there = lax.broadcasted_iota(jnp.int32, (lanes, lanes), 1)
    kpad = table.shape[0]
    by_entry = jnp.where(
        lax.broadcasted_iota(jnp.int32, (lanes, kpad), 0) // REACH == lax.broadcasted_iota(jnp.int32, (lanes, kpad), 1) + 1, 1.0, 0.0)
    by_place = jnp.dot(by_entry, table[...], precision=EXACT, preferred_element_type=f32)
    to_place = jnp.where(here == there // REACH, 1.0, 0.0)
    area = jnp.dot(by_place, to_place, precision=EXACT, preferred_element_type=f32)
    same = here % REACH == there % REACH
    area = jnp.where(same, area, 0.0) * (1.0 / total)
    area_high = area.astype(bf16)
    spread[:, 0:lanes] = area_high
    spread[:, lanes : 2 * lanes] = (area - area_high.astype(f32)).astype(bf16)
    spread[:, 2 * lanes : 3 * lanes] = jnp.where(same & (here < REACH), 1.0, 0.0).astype(bf16)
    gather[...] = jnp.where((here < REACH * bands) & (here % REACH == (there + NEAR) % lanes), 1.0, 0.0).astype(bf16)

    def fill(z, values, to_em, to_1, to_2, to_first, hot):
        if hot:
            t = fourth(values[0])
        for r in range(rows):
            part = slice(r * bands, (r + 1) * bands)
            step = col[0] * values[1][r : r + 1]
            for k in range(1, species):
                step = step + col[k] * values[1 + k][r : r + 1]
            half = [jnp.exp(step * (-0.5 * rate)) for rate in RATES]
            if r:
                for i, to in enumerate((to_1, to_2)):
                    to[z, (r - 1) * bands : r * bands] = last[i] * half[i]
            else:
                for i in range(2):
                    to_first[z, i] = half[i]
            last = half
            to_em[z, part] = step * (share * t[r : r + 1] if hot else share)
        for i, to in enumerate((to_1, to_2)):
            to[z, (rows - 1) * bands : rows * bands] = last[i]

    def fourth(t):
        t = t * t
        return t * t

    def fold(a):
        s = a[0:8]
        for k in range(8, bands, 8):
            s = s + a[k : k + 8]
        return s

    ratio = WEIGHTS[1] / WEIGHTS[0]

    def scan(src, a, b, head):
        zero = jnp.zeros((bands, lanes), f32)

        def part(r):
            return slice(r * bands, (r + 1) * bands)

        def up(z, carry):
            u1, u2, a1, a2 = carry
            for r in range(rows):
                e = src[z, part(r)]
                k1 = a[z, part(r - 1)] if r else a1 * head[z, 0]
                k2 = b[z, part(r - 1)] if r else a2 * head[z, 1]
                u1 = e + k1 * u1
                u2 = ratio * e + k2 * u2
                net[1 + z * rows + r] = fold(u1 + u2)
            return u1, u2, a[z, part(rows - 1)], b[z, part(rows - 1)]

        def down(k, carry):
            d1, d2, a1, a2 = carry
            z = walls - 1 - k
            for r in reversed(range(rows)):
                e, k1, k2 = src[z, part(r)], a[z, part(r)], b[z, part(r)]
                if r == rows - 1:
                    k1, k2 = k1 * a1, k2 * a2
                d1 = e + k1 * d1
                d2 = ratio * e + k2 * d2
                at = 1 + z * rows + r
                net[at] = net[at] - fold(d1 + d2)
            return d1, d2, head[z, 0], head[z, 1]

        loop(walls, up, (zero,) * 4)
        d1, d2, a1, a2 = loop(walls, down, (zero,) * 4)
        net[0] = net[1]
        net[total + 1] = net[total]
        return jnp.sum(fold(a1 * d1 + a2 * d2), axis=0, keepdims=True)

    def halves(a):
        high = a.astype(bf16).astype(f32)
        return jnp.concatenate([high, a - high], axis=0).astype(bf16)

    def fill_edge(z, edge):
        out = jnp.dot(halves(edge), spread[...], preferred_element_type=f32)
        step = out[:rows, :lanes] + out[rows:, :lanes] + out[:rows, lanes : 2 * lanes]
        t = fourth(out[:rows, 2 * lanes :] + out[rows:, 2 * lanes :])
        t1_h[z] = jnp.exp(step * (-0.5 * RATES[0]))
        t2_h[z] = jnp.exp(step * (-0.5 * RATES[1]))
        em_h[z] = step * (share_h * t)

    def edge_flux():
        zero = jnp.zeros((1, lanes), f32)

        def line(z, r):
            return em_h[z, r : r + 1], t1_h[z, r : r + 1], t2_h[z, r : r + 1]

        def up(z, carry):
            u1, u2, a1, a2 = carry
            for r in range(rows):
                e, b1, b2 = line(z, r)
                u1 = e + (a1 * b1) * u1
                u2 = ratio * e + (a2 * b2) * u2
                net_h[1 + z * rows + r] = u1 + u2
                a1, a2 = b1, b2
            return u1, u2, a1, a2

        def down(k, carry):
            d1, d2, a1, a2 = carry
            z = walls - 1 - k
            for r in reversed(range(rows)):
                e, b1, b2 = line(z, r)
                d1 = e + (a1 * b1) * d1
                d2 = ratio * e + (a2 * b2) * d2
                at = 1 + z * rows + r
                net_h[at] = net_h[at] - (d1 + d2)
                a1, a2 = b1, b2
            return d1, d2, a1, a2

        loop(walls, up, (zero,) * 4)
        loop(walls, down, (zero,) * 4)
        net_h[0] = net_h[1]
        net_h[total + 1] = net_h[total]

    def edge_heat():
        at = me * rows
        change = jnp.concatenate([net_h[at + i] - net_h[at + i + 2] for i in range(rows)], axis=0)
        out = jnp.dot(halves(change), gather[...], preferred_element_type=f32)
        return heat_scale * (out[:rows] + out[rows:])

    sub = lax.broadcasted_iota(jnp.int32, (rows, lanes), 0)

    def heat(ref, z):
        at = z * rows
        return row_sums([ref[at + i] - ref[at + i + 2] for i in range(rows)])

    def row_sums(a):
        order = [4 * ((s >> 2) & 1) + 2 * (1 - ((s >> 1) & 1)) + (1 - (s & 1)) for s in range(8)]
        a = [a[order.index(i)] for i in range(8)]
        low = sub < 4
        b = [jnp.where(low, a[i], a[i + 4]) + pltpu.roll(jnp.where(low, a[i + 4], a[i]), 4, 0) for i in range(4)]
        low = (sub & 3) < 2
        c = [
            jnp.where(low, b[i + 2] + pltpu.roll(b[i + 2], rows - 2, 0), b[i] + pltpu.roll(b[i], 2, 0))
            for i in range(2)
        ]
        low = (sub & 1) < 1
        d = jnp.where(low, c[1] + pltpu.roll(c[1], rows - 1, 0), c[0] + pltpu.roll(c[0], 1, 0))
        return heat_scale * d

    def around(x, h):
        s = {0: x}
        for o in (1, 2, 3):
            s[o] = pltpu.roll(jnp.where(lane >= o, x, h), lanes - o, 1)
            s[-o] = pltpu.roll(jnp.where(lane < lanes - o, x, h), o, 1)
        return s

    def tendency(s, cour):
        gradient = (45.0 / 60.0) * (s[1] - s[-1]) - (9.0 / 60.0) * (s[2] - s[-2]) + (1.0 / 60.0) * (s[3] - s[-3])
        smooth = (s[-3] + s[3]) - 6.0 * (s[-2] + s[2]) + 15.0 * (s[-1] + s[1]) - 20.0 * s[0]
        return FILTER * smooth - cour * gradient

    left_half = lane < lanes // 2
    def back(c):
        return (lanes - REACH * c - NEAR) % lanes

    def halo_of(pr, pk, c):
        return jnp.where(left_half, pltpu.roll(pr, back(c), 1), pltpu.roll(pk, back(c), 1))

    def near_of(z):
        return jnp.where(lane % REACH < NEAR, gl[z], gr[z])

    def block(z):
        x = gs[z]
        fill(z, x, em, t1, t2, first_t, True)
        edge = near_of(z)
        h = [pltpu.roll(edge, back(c), 1) for c in range(comps)]
        fill_edge(z, edge)
        cour = gc[z]
        m = [x[c] + tendency(around(x[c], h[c]), cour) for c in range(comps)]
        for c in range(comps):
            ms[z, c] = m[c]
        fill(z, m, em_m, t1_m, t2_m, first_m, False)

    for i in range(2):

        @pl.when(jnp.logical_not(first[i]))
        def _later():
            pl.semaphore_wait(ready.at[1 + i, me], 1)
            edge_copy(i, 0, me).start()

    loop(walls - 1, send_late, 0)
    loop(walls - 1, send_on, 0)
    loop(walls - 1, edges_back, 0)
    loop(walls - 1, rest_back, 0)
    def turn(i):
        if walls != 4:
            return peer(i + 1)
        turns = jnp.where(me == 0, 39, jnp.where(me == 1, 44, jnp.where(me == 2, 28, 18)))
        return (turns >> (2 * i)) & 3

    def arrive(i, _):
        z = jnp.where(i == 0, me, turn(jnp.maximum(i - 1, 0)))
        d = lax.rem(me - z + walls, walls)

        @pl.when(i > 0)
        def _other():
            state_copy(d, z).wait_recv()
            line_copy(d, z).wait_recv()

        for c in edge_copies(d, z):
            c.wait_recv()
        block(z)

        @pl.when(i == 0)
        def _own():
            pr, pk = gr[me], gl[me]
            hc = halo_of(pr, pk, comps)
            cour = gc[me]
            for c in range(comps):
                h = halo_of(pr, pk, c)
                x = gs[me, c]
                mh[c] = h + tendency(around(h, x), hc)
                if c:
                    m = ms[me, c]
                    new_state[c] = 0.5 * (x + m + tendency(around(m, mh[c]), cour))

        return 0

    lax.fori_loop(0, walls, arrive, 0)
    edge_flux()
    flux = scan(em, t1, t2, first_t)
    heat_h = edge_heat()

    def middle(z, _):
        m = ms[z, 0] + heat(net, z)
        ms[z, 0] = m
        t = fourth(m)
        for r in range(rows):
            part = slice(r * bands, (r + 1) * bands)
            em_m[z, part] = em_m[z, part] * t[r : r + 1]
        return 0

    loop(walls, middle, 0)
    flux = flux + scan(em_m, t1_m, t2_m, first_m)
    wall_out[...] = 0.5 * flux
    cour = gc[me]
    m = ms[me, 0]
    h = mh[0] + heat_h
    new_state[0] = 0.5 * (gs[me, 0] + m + tendency(around(m, h), cour) + heat(net, me))

    def finish(i, _):
        nxt = peer(i + 2)

        @pl.when(jnp.logical_not((nxt < me) & (nxt == 1)))
        def _last():
            state_copy(i + 1, me).wait_send()

        line_copy(i + 1, me).wait_send()
        for c in edge_copies(i + 1, me):
            c.wait_send()
        return 0

    loop(walls - 1, finish, 0)
    for c in edge_copies(0, me):
        c.wait_send()


def hand_over(a, b, a_out, b_out, sems):
    copies = [pltpu.make_async_copy(a, a_out, sems.at[0]), pltpu.make_async_copy(b, b_out, sems.at[1])]
    for c in copies:
        c.start()
    for c in copies:
        c.wait()


def local(walls, azims, state, courant, cross_sections, band_fractions, absorb_index, band_index):
    comps, stations, rows, lanes = state.shape
    bands = absorb_index.shape[1]
    species = absorb_index.shape[0]
    entries = cross_sections.shape[0]
    total = rows * walls
    f32 = jnp.float32
    vmem = pltpu.VMEM
    dma = pltpu.SemaphoreType.DMA
    hbm_spec = pl.BlockSpec(memory_space=pltpu.HBM)
    vmem_spec = pl.BlockSpec(memory_space=pltpu.VMEM)
    new_state, wall = pl.pallas_call(
        functools.partial(kernel, walls, azims),
        out_shape=(
            pltpu.VMEM((comps, rows, lanes), f32),
            pltpu.VMEM((1, lanes), f32),
        ),
        in_specs=[hbm_spec] * 6,
        out_specs=(vmem_spec, vmem_spec),
        scratch_shapes=[
            vmem((walls, comps, rows, lanes), f32),
            vmem((walls, rows, lanes), f32),
            vmem((walls, rows, lanes), f32),
            vmem((walls, rows, lanes), f32),
            vmem((walls, comps, rows, lanes), f32),
            vmem((comps, rows, lanes), f32),
            vmem((rows, lanes), f32),
            vmem((rows, lanes), f32),
        ] + [vmem((walls, rows * bands, lanes), f32)] * 3 + [vmem((walls, rows, lanes), f32)] * 3 + [
            vmem((walls, rows * bands, lanes), f32)] * 3 + [vmem((walls, 2, bands, lanes), f32)] * 2 + [
            vmem((total + 2, 8, lanes), f32),
            vmem((total + 2, 1, lanes), f32),
            vmem((16, lanes), f32),
            vmem((species, bands, lanes), f32),
            vmem((lanes, 3 * lanes), jnp.bfloat16),
            vmem((lanes, lanes), jnp.bfloat16),
            vmem((species, bands), jnp.int32),
            pltpu.SMEM((entries,), f32),
            pltpu.SMEM((entries,), f32),
            pltpu.SMEM((bands,), jnp.int32),
            dma((6,)),
        ] + [dma((walls,))] * 4 + [dma((2, walls))] * 2 + [pltpu.SemaphoreType.REGULAR((3, walls))],
        compiler_params=pltpu.CompilerParams(
            collective_id=0, has_side_effects=True, vmem_limit_bytes=58 * 1024 * 1024),
    )(state.reshape(comps, rows, lanes), courant.reshape(rows, lanes), cross_sections, band_fractions, absorb_index, band_index)
    hbm = pl.BlockSpec(memory_space=pltpu.HBM)
    new_state, wall = pl.pallas_call(
        hand_over,
        out_shape=(
            jax.ShapeDtypeStruct((comps, rows, lanes), f32),
            jax.ShapeDtypeStruct((1, lanes), f32),
        ),
        in_specs=[pl.BlockSpec(memory_space=pl.ANY)] * 2,
        out_specs=(hbm, hbm),
        scratch_shapes=[dma((2,))],
    )(pltpu.with_memory_space_constraint(new_state, pltpu.VMEM), pltpu.with_memory_space_constraint(wall, pltpu.VMEM))
    return new_state.reshape(state.shape), wall


def solution(mesh):
    return jax.shard_map(
        functools.partial(local, mesh.shape["wall"], mesh.shape["azim"]),
        mesh=mesh,
        in_specs=(P(None, "case", "wall", "azim"), P("case", "wall", "azim"), P(), P(), P(), P()),
        out_specs=(P(None, "case", "wall", "azim"), P("case", "azim")),
        check_vma=False,
    )
```
